512 devices in a mesh: gx: 8 (over x, core), gy: 8 (over z), gz: 8 (over y).
Axes of the slice: x: 4, y: 8, z: 8, core: 2. Of those that a mesh axis runs over, the one named last changes fastest.
Arguments:
- prior_basis: float32 [32, 128, 12288], P('gx', 'gy', 'gz'), may hold values from -6 to 6
- edge_weights: float32 [3, 32, 128, 128], P(None, 'gx', 'gy', 'gz'), may hold values from 0.5 to 1.5
- spectral_shift: float32 [1], replicated, may hold values from 0.5 to 4
Outputs:
- new_basis: float32 [32, 128, 16384], P('gx', 'gy', 'gz')
- projection: float32 [96, 128], replicated
- triangle: float32 [128, 128], replicated
The draws below stay inside these ranges and needn't reach their ends.
All inputs are finite; a program needn't handle non-finite values.
Results may differ from the reference program's by a relative error of at most 0.002.
Values sent between devices are 32-bit elements; how exact they have to be, the bound alone decides.
A program may use at most 64 MiB of HBM per device.

```python
import math
import jax
import jax.numpy as jnp
from jax import lax

BLOCK = 32
POWERS = 4
PRIOR = 3
BASIS = 96
NX = 32
NY = 128
NZ = 128


def draw_prior_basis(key, part):
    key_own = jax.random.fold_in(key, 11)
    key_shared = jax.random.fold_in(key, 12)
    own_part = jnp.clip(jax.random.normal(key_own, (NX, NY, NZ, PRIOR, BLOCK), jnp.float32), -4.0, 4.0)
    shared_part = jnp.clip(jax.random.normal(key_shared, (NX, NY, NZ, 1, BLOCK), jnp.float32), -4.0, 4.0)
    mixed = own_part + 0.15 * shared_part
    return mixed.reshape(NX, NY, NZ * PRIOR * BLOCK)


def steps_of(own_key, shape, cuts, low, high):
    gain, own = 1.0, jax.random.fold_in(own_key, 6)
    for axis_at, blocks in cuts:
        draws = jnp.exp(jax.random.uniform(jax.random.fold_in(own, axis_at), (blocks,), jnp.float32, low / len(cuts), high / len(cuts)))
        gain = gain * jnp.repeat(draws, shape[axis_at] // blocks).reshape([-1 if axis == axis_at else 1 for axis in range(len(shape))])
    return gain


def setup_inputs(seed: int = 0) -> dict:
    arg_keys = jax.random.split(jax.random.key(seed), 4)
    prior_basis = draw_prior_basis(jax.random.fold_in(arg_keys[3], 71), 0)
    edge_weights = jnp.clip(jnp.exp(math.log(1.5) - 1.0986123 * jax.random.uniform(arg_keys[1], (3, NX, NY, NZ), jnp.float32) ** steps_of(arg_keys[1], (3, NX, NY, NZ), ((1, 8), (2, 8), (3, 8)), -0.2, 0.2)), 0.5, 1.5)
    spectral_shift = jnp.clip(jnp.exp(jax.random.uniform(arg_keys[2], (1,), jnp.float32, math.log(0.5), math.log(4.0))), 0.5, 4.0)
    return {"prior_basis": prior_basis, "edge_weights": edge_weights, "spectral_shift": spectral_shift}


PRECISE = lax.Precision.HIGHEST
OPERATOR_SCALE = 11.0

def apply_operator(field, weight_pad, shift_value):
    padded = jnp.pad(field, ((1, 1), (1, 1), (1, 1), (0, 0)))
    centre = field
    summed = weight_pad[0, 1:-1, 1:-1, 1:-1] * (centre - padded[2:, 1:-1, 1:-1]) + weight_pad[0, :-2, 1:-1, 1:-1] * (centre - padded[:-2, 1:-1, 1:-1])
    summed = summed + weight_pad[1, 1:-1, 1:-1, 1:-1] * (centre - padded[1:-1, 2:, 1:-1]) + weight_pad[1, 1:-1, :-2, 1:-1] * (centre - padded[1:-1, :-2, 1:-1])
    summed = summed + weight_pad[2, 1:-1, 1:-1, 1:-1] * (centre - padded[1:-1, 1:-1, 2:]) + weight_pad[2, 1:-1, 1:-1, :-2] * (centre - padded[1:-1, 1:-1, :-2])
    return (summed + shift_value * centre) / OPERATOR_SCALE - centre

def reference(prior_basis, edge_weights, spectral_shift):
    cell_count = NX * NY * NZ
    basis_rows = prior_basis.reshape(cell_count, BASIS)
    start_block = prior_basis.reshape(NX, NY, NZ, BASIS)[..., BASIS - BLOCK:]
    weight_pad = jnp.pad(edge_weights, ((0, 0), (1, 1), (1, 1), (1, 1)))[..., None]
    shift_value = spectral_shift[0]
    previous = start_block
    current = apply_operator(start_block, weight_pad, shift_value)
    powers = [current]
    for degree in range(1, POWERS):
        following = 2.0 * apply_operator(current, weight_pad, shift_value) - previous
        previous, current = (current, following)
        powers.append(following)
    krylov = jnp.stack(powers, axis=3).reshape(cell_count, BLOCK * POWERS)
    first_coef = jnp.dot(basis_rows.T, krylov, precision=PRECISE) / cell_count
    once = krylov - jnp.dot(basis_rows, first_coef, precision=PRECISE)
    second_coef = jnp.dot(basis_rows.T, once, precision=PRECISE) / cell_count
    twice = once - jnp.dot(basis_rows, second_coef, precision=PRECISE)
    gram_matrix = jnp.dot(twice.T, twice, precision=PRECISE) / cell_count
    lower_factor = jnp.linalg.cholesky(gram_matrix)
    solved = jax.scipy.linalg.solve_triangular(lower_factor, twice.T, lower=True)
    new_basis = solved.T.reshape(NX, NY, NZ * BLOCK * POWERS)
    return (new_basis, first_coef + second_coef, lower_factor.T)
```

```python
import functools
import jax
import jax.numpy as jnp
from jax import lax
from jax.experimental import pallas as pl
from jax.experimental.pallas import tpu as pltpu
from jax.sharding import PartitionSpec as P

BLOCK = 32
POWERS = 4
BASIS = 96
LANES = 128
OPERATOR_SCALE = 11.0
CENTRE = 6.0
WIDTH = 2.5
MESH = pl.DeviceIdType.MESH
AXES = ("gx", "gy", "gz")
V_LANE = (64, 32, 0, 96)
V_TILE = (0, 1, 2, 2)


def roll_lanes(values, shift):
    return values if shift % LANES == 0 else pltpu.roll(values, shift % LANES, axis=values.ndim - 1)


def tree_sum(parts):
    while len(parts) > 1:
        parts = [parts[i] + parts[i + 1] for i in range(0, len(parts), 2)]
    return parts[0]


def powers_kernel(
    sizes,
    q_ref,
    w_ref,
    total_ref,
    xa_ref,
    xb_ref,
    field,
    weight,
    coef,
    halo_x,
    halo_y,
    halo_z,
    face_y,
    edge_x,
    edge_y,
    edge_z,
    face_wy,
    local_sum,
    part_x,
    send_z,
    part_z,
    send_y,
    part_y,
    send_x,
    halo_send,
    halo_recv,
    edge_send,
    edge_recv,
    sum_send,
    sum_recv,
):
    nx, ny, nz = sizes
    at = dict(zip(AXES, (lax.axis_index(a) for a in AXES)))
    gx, gy, gz = at["gx"], at["gy"], at["gz"]
    size_of = dict(zip(AXES, sizes))

    def moved(axis, index):
        return tuple(index if a == axis else at[a] for a in AXES)

    def beside(axis, step):
        n = size_of[axis]
        return moved(axis, lax.rem(at[axis] + (n + step), n))

    def partner(axis, d):
        return moved(axis, at[axis] ^ d)

    barrier = pltpu.get_barrier_semaphore()
    peers = 0
    for axis in AXES:
        for d in range(1, size_of[axis]):
            pl.semaphore_signal(barrier, inc=1, device_id=partner(axis, d), device_id_type=MESH)
            peers += 1

    lane = lax.broadcasted_iota(jnp.int32, (16, LANES), 1)
    row = lax.broadcasted_iota(jnp.int32, (16, LANES), 0)
    group = lane // BLOCK

    def by_group(parts):
        out = parts[0]
        for g in range(1, 4):
            out = jnp.where(group == g, parts[g], out)
        return out

    def q_tile(i, n):
        return q_ref[i, :, n * LANES : (n + 1) * LANES]

    def put(level, i, t, value):
        field[level, i, t] = value
        if level < POWERS:
            face_y[level, 0, 4 * i + t : 4 * i + t + 1, :] = value[15:16, :]
            face_y[level, 1, 4 * i + t : 4 * i + t + 1, :] = value[0:1, :]

    for i in range(4):
        for t in range(4):
            put(
                0,
                i,
                t,
                by_group([roll_lanes(q_tile(i, 3 * g + V_TILE[t]), BLOCK * g - V_LANE[t]) for g in range(4)]),
            )

    spread_k = lax.broadcasted_iota(jnp.int32, (16, 4 * LANES), 0)
    spread_lane = lax.broadcasted_iota(jnp.int32, (16, 4 * LANES), 1)
    spread = (spread_k == 4 * ((spread_lane % LANES) // BLOCK) + spread_lane // LANES).astype(jnp.float32)
    wide = jnp.dot(
        w_ref[...].reshape(192, 16), spread, precision=lax.Precision.HIGHEST, preferred_element_type=jnp.float32
    )
    for d in range(3):
        for i in range(4):
            for t in range(4):
                r = 16 * (4 * d + i)
                value = wide[r : r + 16, t * LANES : (t + 1) * LANES] * (1.0 / WIDTH)
                weight[d, i, t] = value
                if d == 1:
                    face_wy[4 * i + t : 4 * i + t + 1, :] = value[15:16, :]

    pl.semaphore_wait(barrier, peers)

    def halo_copies(level):
        def copy(src, dst, n, device):
            return pltpu.make_async_remote_copy(
                src_ref=src,
                dst_ref=dst,
                send_sem=halo_send.at[level, n],
                recv_sem=halo_recv.at[level, n],
                device_id=device,
                device_id_type=MESH,
            )

        return [
            copy(field.at[level, 3], halo_x.at[level, 0], 0, beside("gx", 1)),
            copy(field.at[level, 0], halo_x.at[level, 1], 1, beside("gx", -1)),
            copy(field.at[level, :, 3], halo_z.at[level, 0], 2, beside("gz", 1)),
            copy(field.at[level, :, 0], halo_z.at[level, 1], 3, beside("gz", -1)),
            copy(face_y.at[level, 0], halo_y.at[level, 0], 4, beside("gy", 1)),
            copy(face_y.at[level, 1], halo_y.at[level, 1], 5, beside("gy", -1)),
        ]

    def edge_copy(src, dst, n, axis):
        return pltpu.make_async_remote_copy(
            src_ref=src,
            dst_ref=dst,
            send_sem=edge_send.at[n],
            recv_sem=edge_recv.at[n],
            device_id=beside(axis, 1),
            device_id_type=MESH,
        )

    edges = [
        edge_copy(weight.at[0, 3], edge_x, 0, "gx"),
        edge_copy(weight.at[2, :, 3], edge_z, 1, "gz"),
        edge_copy(face_wy, edge_y, 2, "gy"),
    ]
    rounds = [halo_copies(level) for level in range(POWERS)]
    for copy in edges + rounds[0]:
        copy.start()

    def place_basis():
        for i in range(4):
            for g in range(4):
                a, b, c = (q_tile(i, 3 * g + n) for n in range(3))
                parts = [
                    a,
                    roll_lanes(jnp.where(lane >= 96, a, b), 32),
                    roll_lanes(jnp.where(lane >= 64, b, c), 64),
                    roll_lanes(c, 96),
                ]
                for t in range(4):
                    xa_ref[4 * g + t, 16 * i : 16 * i + 16, :] = parts[t]

    place_basis()

    for copy in edges:
        copy.wait_recv()
    low_x, high_x = gx > 0, gx < nx - 1
    low_y, high_y = gy > 0, gy < ny - 1
    low_z, high_z = gz > 0, gz < nz - 1

    def kept(flag):
        return jnp.where(flag, 1.0, 0.0).astype(jnp.float32)

    for i in range(4):
        for t in range(4):
            xp, yp, zp = weight[0, i, t], weight[1, i, t], weight[2, i, t]
            xm = weight[0, i - 1, t] if i > 0 else edge_x[t] * kept(low_x)
            ym = jnp.where(
                row == 0, edge_y[4 * i + t : 4 * i + t + 1, :] * kept(low_y), pltpu.roll(yp, 1, axis=0)
            )
            if t > 0:
                zm = weight[2, i, t - 1]
            else:
                zm = jnp.where(
                    group == 0, roll_lanes(edge_z[i], 32) * kept(low_z), roll_lanes(weight[2, i, 3], 32)
                )
            coef[0, i, t] = ((xp + xm) + (yp + ym)) + (zp + zm) - CENTRE / WIDTH
            coef[1, i, t] = xp * kept(high_x) if i == 3 else xp
            coef[2, i, t] = xm
            coef[3, i, t] = jnp.where(row == 15, yp * kept(high_y), yp)
            coef[4, i, t] = ym
            coef[5, i, t] = jnp.where(group == 3, zp * kept(high_z), zp) if t == 3 else zp
            coef[6, i, t] = zm

    for level in range(POWERS):
        for copy in rounds[level]:
            copy.wait_recv()
        for i in range(4):
            for t in range(4):
                centre = field[level, i, t]
                xp = field[level, i + 1, t] if i < 3 else halo_x[level, 1, t]
                xm = field[level, i - 1, t] if i > 0 else halo_x[level, 0, t]
                r = 4 * i + t
                yp = jnp.where(row == 15, halo_y[level, 1, r : r + 1, :], pltpu.roll(centre, 15, axis=0))
                ym = jnp.where(row == 0, halo_y[level, 0, r : r + 1, :], pltpu.roll(centre, 1, axis=0))
                if t < 3:
                    zp = field[level, i, t + 1]
                else:
                    zp = roll_lanes(jnp.where(group == 0, halo_z[level, 1, i], field[level, i, 0]), 96)
                if t > 0:
                    zm = field[level, i, t - 1]
                else:
                    zm = roll_lanes(jnp.where(group == 3, halo_z[level, 0, i], field[level, i, 3]), 32)
                value = coef[0, i, t] * centre
                value = value - (coef[1, i, t] * xp + coef[2, i, t] * xm)
                value = value - (coef[3, i, t] * yp + coef[4, i, t] * ym)
                value = value - (coef[5, i, t] * zp + coef[6, i, t] * zm)
                if level > 0:
                    value = value - field[level - 1, i, t]
                put(level + 1, i, t, value)
        if level + 1 < POWERS:
            for copy in rounds[level + 1]:
                copy.start()

    zero = jnp.zeros((16, LANES), jnp.float32)
    for i in range(4):
        for g in range(4):
            for t in range(4):
                k = 4 * g + t
                rows = slice(16 * i, 16 * i + 16)
                pieces = [roll_lanes(field[m + 1, i, t], BLOCK * (m - g)) for m in range(4)]
                xa_ref[k, rows, :] = jnp.where(group == 3, pieces[3], xa_ref[k, rows, :])
                xb_ref[k, rows, :] = by_group(pieces[:3] + [zero])

    xa = xa_ref[...].reshape(1024, LANES)
    xb = xb_ref[...].reshape(1024, LANES)
    both = jnp.concatenate([xa, xb], axis=1)
    gram = lax.dot_general(
        xa,
        both,
        (((0,), (0,)), ((), ())),
        precision=lax.Precision.HIGH,
        preferred_element_type=jnp.float32,
    )
    chunk = LANES // nx
    for c in range(nx):
        local_sum[c] = gram[c * chunk : (c + 1) * chunk, :]

    def sum_copy(src, dst, n, device):
        return pltpu.make_async_remote_copy(
            src_ref=src,
            dst_ref=dst,
            send_sem=sum_send.at[n],
            recv_sem=sum_recv.at[n],
            device_id=device,
            device_id_type=MESH,
        )

    for d in range(1, nx):
        sum_copy(local_sum.at[gx ^ d], part_x.at[d], 0, partner("gx", d)).start()
    part_x[0] = local_sum[gx]
    all_x = sum_copy(part_x.at[pl.ds(1, nx - 1)], part_x.at[pl.ds(1, nx - 1)], 0, partner("gx", 1))
    all_x.wait_recv()
    send_z[...] = tree_sum([part_x[d] for d in range(nx)])
    for d in range(1, nz):
        sum_copy(send_z, part_z.at[d], 1, partner("gz", d)).start()
    all_z = sum_copy(part_z.at[pl.ds(1, nz - 1)], part_z.at[pl.ds(1, nz - 1)], 1, partner("gz", 1))
    all_z.wait_recv()
    send_y[...] = tree_sum([send_z[...]] + [part_z[d] for d in range(1, nz)])
    for d in range(1, ny):
        sum_copy(send_y, part_y.at[d], 2, partner("gy", d)).start()
    all_y = sum_copy(part_y.at[pl.ds(1, ny - 1)], part_y.at[pl.ds(1, ny - 1)], 2, partner("gy", 1))
    all_y.wait_recv()
    whole = tree_sum([send_y[...]] + [part_y[d] for d in range(1, ny)])
    send_x[...] = whole
    for d in range(1, nx):
        sum_copy(send_x, total_ref.at[gx], 3, partner("gx", d)).start()
    total_ref[gx] = whole
    last = sum_copy(total_ref.at[pl.ds(0, nx - 1)], total_ref.at[pl.ds(0, nx - 1)], 3, partner("gx", 1))
    last.wait_recv()

    for copy in edges + [c for r in rounds for c in r]:
        copy.wait_send()
    for copy in (all_x, all_z, all_y, last):
        copy.wait_send()


def basis_kernel(cells, total_ref, xa_ref, xb_ref, shift_ref, new_ref, projection_ref, triangle_ref, factor, inverse):
    exact = functools.partial(
        lax.dot_general, precision=lax.Precision.HIGHEST, preferred_element_type=jnp.float32
    )

    def mm(a, b):
        return exact(a, b, (((1,), (0,)), ((), ())))

    alpha = WIDTH / OPERATOR_SCALE
    beta = (shift_ref[0] + CENTRE) / OPERATOR_SCALE - 1.0
    t = [[1.0, 0.0, 0.0, 0.0, 0.0], [beta, alpha, 0.0, 0.0, 0.0]]
    for k in range(1, POWERS):
        p, before = t[k], t[k - 1]
        nxt = []
        for j in range(5):
            if j > k + 1:
                nxt.append(0.0)
                continue
            shifted = (p[j - 1] if j > 0 else 0.0) + (p[j + 1] if j < 4 else 0.0)
            nxt.append(2.0 * (alpha * shifted + beta * p[j]) - before[j])
        t.append(nxt)
    tau = []
    for k in range(1, POWERS + 1):
        rest = t[k][0]
        for j in range(1, k):
            rest = rest - t[k][j] * tau[j - 1]
        tau.append(rest * (1.0 / (alpha * (2.0 * alpha) ** (k - 1))))

    def lanes_of(shape):
        return lax.broadcasted_iota(jnp.int32, shape, 1)

    def by_group(shape, values, dim=1):
        which = lax.broadcasted_iota(jnp.int32, shape, dim) // BLOCK
        out = jnp.full(shape, values[0], jnp.float32)
        for n in range(1, 4):
            out = jnp.where(which == n, values[n], out)
        return out

    scale = 1.0 / cells
    left = total_ref[...].reshape(LANES, 2 * LANES)[:, :LANES] * scale
    right = total_ref[...].reshape(LANES, 2 * LANES)[:, LANES:] * scale
    merged = jnp.where(lanes_of((LANES, LANES)) < BASIS, right, left)
    gram_q = left[:BASIS, :]
    coef = merged[:BASIS, :]
    last = merged[BASIS:, :]

    strip = lanes_of((BLOCK, LANES))
    rows = [coef[64:96, :]]
    moment = [roll_lanes(gram_q[64:96, :], 64)] + [roll_lanes(rows[0], -BLOCK * m) for m in range(3)]
    for j in range(POWERS - 1):
        up = roll_lanes(rows[j], -BLOCK)
        down = jnp.where(strip < BLOCK, moment[j], roll_lanes(rows[j], BLOCK))
        nxt = up + down
        if j > 0:
            nxt = nxt - rows[j - 1]
        rows.append(jnp.where(strip < BASIS, nxt, roll_lanes(last, BASIS - BLOCK * j)))
    gram_b = jnp.concatenate(rows[1:] + [last], axis=0)

    wide = lanes_of((BASIS, LANES))
    tall = lax.broadcasted_iota(jnp.int32, (BASIS, LANES), 0)
    off = jnp.where(wide < BASIS, jnp.where(wide == tall, 1.0, 0.0) - gram_q, 0.0)
    e1 = off[:, :BASIS]
    first = mm(e1, jnp.concatenate([off, coef], axis=1))
    square, c2 = first[:, :LANES], first[:, LANES:]
    e2 = square[:, :BASIS]
    second = mm(e2, jnp.concatenate([coef, c2, square], axis=1))
    c3, c4, fourth = second[:, :LANES], second[:, LANES : 2 * LANES], second[:, 2 * LANES :]
    left_over = mm(fourth[64:96, :BASIS], jnp.concatenate([coef, gram_q], axis=1))
    over_b, over_v = left_over[:, :LANES], left_over[:, LANES:]
    gram = gram_b - exact(coef, (coef + c2) + (c3 + c4), (((0,), (0,)), ((), ())))
    over_v = roll_lanes(over_v, -64)
    over_v = jnp.where(strip < BLOCK, over_v, 0.0)
    over_v = (over_v + roll_lanes(over_v, 32)) + (roll_lanes(over_v, 64) + roll_lanes(over_v, 96))
    half = over_b + (0.5 * by_group((BLOCK, LANES), tau)) * over_v
    half = jnp.concatenate([tau[n] * half for n in range(4)], axis=0)
    gram = gram + (half + half.T)

    sub = lax.broadcasted_iota(jnp.int32, (8, LANES), 0)
    lane8 = lanes_of((8, LANES))
    a = [gram[8 * b : 8 * b + 8, :] for b in range(16)]
    z = [jnp.where(lane8 == sub + 8 * b, 1.0, 0.0) for b in range(16)]
    for j in range(LANES):
        b0, s = divmod(j, 8)
        row_a, row_z = a[b0][s : s + 1, :], z[b0][s : s + 1, :]
        pivot = row_a[:, j : j + 1]
        root = lax.rsqrt(pivot)
        row_a, row_z = row_a * root, row_z * root
        factor[j : j + 1, :] = row_a
        inverse[j : j + 1, :] = row_z
        for b in range(b0, 16):
            if b == b0 and s == 7:
                continue
            column = a[b][:, j : j + 1] * root
            if b == b0:
                column = jnp.where(sub > s, column, 0.0)
            a[b] = a[b] - column * row_a
            z[b] = z[b] - column * row_z

    square_lane = lanes_of((LANES, LANES))
    square_row = lax.broadcasted_iota(jnp.int32, (LANES, LANES), 0)
    upper = jnp.where(square_lane >= square_row, factor[...], 0.0)
    lower_inverse = jnp.where(square_lane <= square_row, inverse[...], 0.0)

    t_rows = [by_group((LANES, LANES), [t[k][j] for k in range(1, 5)]) for j in range(1, 5)]
    which = square_row // BLOCK
    mixing = t_rows[0]
    for n in range(1, 4):
        mixing = jnp.where(which == n, t_rows[n], mixing)
    mixing = jnp.where(square_row % BLOCK == square_lane % BLOCK, mixing, 0.0)
    triangle_ref[...] = jnp.where(square_lane >= square_row, mm(upper, mixing), 0.0)

    twice = coef + c2
    leak = jnp.where(wide < BLOCK, roll_lanes(square, -64), 0.0)
    leak = (leak + roll_lanes(leak, 32)) + (roll_lanes(leak, 64) + roll_lanes(leak, 96))
    unit = jnp.where(tall - 64 == wide % BLOCK, 1.0, 0.0)
    projection_ref[...] = mm(twice, mixing) + by_group((BASIS, LANES), [t[k][0] for k in range(1, 5)]) * (unit - leak)

    back = leak * by_group((BASIS, LANES), tau) - twice
    back = exact(back, lower_inverse, (((1,), (1,)), ((), ())))
    upper_inverse = lower_inverse.T
    maps = jnp.concatenate([back, upper_inverse[BASIS:, :], upper_inverse], axis=0)
    for k in range(16):
        both = jnp.concatenate([xa_ref[k], xb_ref[k]], axis=1)
        out = lax.dot_general(
            both,
            maps,
            (((1,), (0,)), ((), ())),
            precision=lax.Precision.HIGH,
            preferred_element_type=jnp.float32,
        )
        for i in range(4):
            new_ref[i, :, k * LANES : (k + 1) * LANES] = out[16 * i : 16 * i + 16, :]


def per_device(sizes, prior_basis, edge_weights, spectral_shift):
    nx, ny, nz = sizes
    f32 = jnp.float32
    chunk = LANES // nx
    piece = (chunk, 2 * LANES)
    vmem = pl.BlockSpec(memory_space=pltpu.VMEM)
    total, xa, xb = pl.pallas_call(
        functools.partial(powers_kernel, sizes),
        out_shape=(
            jax.ShapeDtypeStruct((nx, *piece), f32),
            jax.ShapeDtypeStruct((16, 64, LANES), f32),
            jax.ShapeDtypeStruct((16, 64, LANES), f32),
        ),
        in_specs=[vmem, vmem],
        out_specs=(vmem, vmem, vmem),
        scratch_shapes=[
            pltpu.VMEM((POWERS + 1, 4, 4, 16, LANES), f32),
            pltpu.VMEM((3, 4, 4, 16, LANES), f32),
            pltpu.VMEM((7, 4, 4, 16, LANES), f32),
            pltpu.VMEM((POWERS, 2, 4, 16, LANES), f32),
            pltpu.VMEM((POWERS, 2, 16, LANES), f32),
            pltpu.VMEM((POWERS, 2, 4, 16, LANES), f32),
            pltpu.VMEM((POWERS, 2, 16, LANES), f32),
            pltpu.VMEM((4, 16, LANES), f32),
            pltpu.VMEM((16, LANES), f32),
            pltpu.VMEM((4, 16, LANES), f32),
            pltpu.VMEM((16, LANES), f32),
            pltpu.VMEM((nx, *piece), f32),
            pltpu.VMEM((nx, *piece), f32),
            pltpu.VMEM(piece, f32),
            pltpu.VMEM((nz, *piece), f32),
            pltpu.VMEM(piece, f32),
            pltpu.VMEM((ny, *piece), f32),
            pltpu.VMEM(piece, f32),
            pltpu.SemaphoreType.DMA((POWERS, 6)),
            pltpu.SemaphoreType.DMA((POWERS, 6)),
            pltpu.SemaphoreType.DMA((3,)),
            pltpu.SemaphoreType.DMA((3,)),
            pltpu.SemaphoreType.DMA((4,)),
            pltpu.SemaphoreType.DMA((4,)),
        ],
        name="powers",
        compiler_params=pltpu.CompilerParams(
            collective_id=0, has_side_effects=True, vmem_limit_bytes=32 * 2**20
        ),
    )(prior_basis, edge_weights)
    cells = 1024 * nx * ny * nz
    return pl.pallas_call(
        functools.partial(basis_kernel, cells),
        out_shape=(
            jax.ShapeDtypeStruct((4, 16, 16 * LANES), f32),
            jax.ShapeDtypeStruct((BASIS, LANES), f32),
            jax.ShapeDtypeStruct((LANES, LANES), f32),
        ),
        in_specs=[vmem, vmem, vmem, pl.BlockSpec(memory_space=pltpu.SMEM)],
        out_specs=(vmem, vmem, vmem),
        scratch_shapes=[pltpu.VMEM((LANES, LANES), f32), pltpu.VMEM((LANES, LANES), f32)],
        name="basis",
        compiler_params=pltpu.CompilerParams(vmem_limit_bytes=32 * 2**20),
    )(total, xa, xb, spectral_shift)


def solution(mesh):
    sizes = tuple(mesh.shape[a] for a in AXES)
    return jax.shard_map(
        functools.partial(per_device, sizes),
        mesh=mesh,
        in_specs=(P("gx", "gy", "gz"), P(None, "gx", "gy", "gz"), P()),
        out_specs=(P("gx", "gy", "gz"), P(), P()),
        check_vma=False,
    )
```

```python
import functools
import jax
import jax.numpy as jnp
from jax import lax
from jax.experimental import pallas as pl
from jax.experimental.pallas import tpu as pltpu
from jax.sharding import PartitionSpec as P

BLOCK = 32
POWERS = 4
BASIS = 96
LANES = 128
OPERATOR_SCALE = 11.0
CENTRE = 6.0
WIDTH = 2.5
MESH = pl.DeviceIdType.MESH
AXES = ("gx", "gy", "gz")
V_LANE = (64, 32, 0, 96)
V_TILE = (0, 1, 2, 2)


def roll_lanes(values, shift):
    return values if shift % LANES == 0 else pltpu.roll(values, shift % LANES, axis=values.ndim - 1)


def tree_sum(parts):
    while len(parts) > 1:
        parts = [parts[i] + parts[i + 1] for i in range(0, len(parts), 2)]
    return parts[0]


def exact(a, b, dims):
    return lax.dot_general(
        a, b, (dims, ((), ())), precision=lax.Precision.HIGHEST, preferred_element_type=jnp.float32
    )


def mm(a, b):
    return exact(a, b, ((1,), (0,)))


def mm_t(a, b):
    return exact(a, b, ((1,), (1,)))


def lanes_of(shape):
    return lax.broadcasted_iota(jnp.int32, shape, 1)


def rows_of(shape):
    return lax.broadcasted_iota(jnp.int32, shape, 0)


def by_block(shape, values, dim=1):
    which = lax.broadcasted_iota(jnp.int32, shape, dim) // BLOCK
    out = jnp.full(shape, values[0], jnp.float32)
    for n in range(1, 4):
        out = jnp.where(which == n, values[n], out)
    return out


def pick(parts):
    shape = next(p.shape for p in parts if p is not None)
    which = lanes_of(shape) // BLOCK
    out = jnp.zeros(shape, jnp.float32)
    for n, p in enumerate(parts):
        if p is not None:
            out = jnp.where(which == n, p, out)
    return out


def spread_block(values, block):
    own = jnp.where(lanes_of(values.shape) // BLOCK == block, values, 0.0)
    own = own + roll_lanes(own, 32)
    return own + roll_lanes(own, 64)


def scalars(shift):
    alpha = WIDTH / OPERATOR_SCALE
    beta = (shift + CENTRE) / OPERATOR_SCALE - 1.0
    t = [[1.0, 0.0, 0.0, 0.0, 0.0], [beta, alpha, 0.0, 0.0, 0.0]]
    for k in range(1, POWERS):
        p, before = t[k], t[k - 1]
        row = []
        for j in range(5):
            if j > k + 1:
                row.append(0.0)
                continue
            shifted = (p[j - 1] if j > 0 else 0.0) + (p[j + 1] if j < 4 else 0.0)
            row.append(2.0 * (alpha * shifted + beta * p[j]) - before[j])
        t.append(row)
    tau = []
    for k in range(1, POWERS + 1):
        rest = t[k][0]
        for j in range(1, k):
            rest = rest - t[k][j] * tau[j - 1]
        tau.append(rest * (1.0 / (alpha * (2.0 * alpha) ** (k - 1))))
    return t, tau


def prior_algebra(gram, tau):
    shape = (LANES, LANES)
    lane, row = lanes_of(shape), rows_of(shape)
    inside = (lane >= BLOCK) & (row >= BLOCK)
    prior = jnp.where(inside, gram, 0.0)
    unit = jnp.where(inside & (lane == row), 1.0, 0.0)
    off = unit - prior
    off2 = mm(off, off)
    high = mm(off2, jnp.concatenate([off, off2], axis=1))
    off3, off4 = high[:, :LANES], high[:, LANES:]
    series = (unit + off) + (off2 + off3)
    tau_row = by_block((1, LANES), tau)
    right = jnp.concatenate([series, spread_block(off4, 1) * tau_row, unit + off], axis=1)
    over = off4[32:64, :]
    over_v = mm(over, spread_block(prior, 1) * tau_row)
    return dict(right=right, over=over, over_v=over_v, off2=off2)


def level_algebra(m, products, p, done, prior, tau, eliminate):
    strip = (BLOCK, LANES)
    lane, row = lanes_of(strip), rows_of(strip)
    p[2 * m] = (products, 0)
    p[2 * m - 1] = (products, 1)

    def at(n, block):
        values, own = p[n]
        return roll_lanes(values, BLOCK * (block - own))

    moment = at(m, 1) - at(m - 2, 1) if m > 1 else at(1, 1)
    coef = pick([None, moment, products, products])
    mixed = mm(coef, prior["right"])
    series, over, twice = mixed[:, :LANES], mixed[:, LANES : 2 * LANES], mixed[:, 2 * LANES :]
    blocks = [None] * 4
    for k in range(1, m + 1):
        value = at(m + k, k - 1)
        if m - k >= 2:
            value = value - at(m - k - 2, k - 1)
        blocks[k - 1] = value
    nothing = jnp.zeros(strip, jnp.float32)

    def column(name, own):
        parts = done[name] + [own]
        return jnp.concatenate(parts + [nothing] * (4 - len(parts)), axis=0)

    coefs = column("coef", coef)
    inverse = column("inverse", nothing)
    gram = pick(blocks) + over + tau[m - 1] * prior["over_v"]
    gram = gram + mm_t(tau[m - 1] * prior["over"] - series, coefs)
    below = roll_lanes(gram, -BLOCK * (m - 1))
    if m > 1:
        factor = mm_t(gram, inverse)
        pad = jnp.concatenate([factor] + [nothing] * 3, axis=0)
        below = below - mm_t(factor, pad)
        product = mm(factor, inverse)
    work = jnp.where(lane < BLOCK, below, jnp.where(lane == row + BLOCK, 1.0, 0.0))
    work = eliminate(work)
    upper = jnp.where((lane < BLOCK) & (lane >= row), work, 0.0)
    lower = jnp.where((lane >= BLOCK) & (lane <= row + BLOCK), work, 0.0)
    inverse_row = roll_lanes(lower, BLOCK * (m - 2))
    if m > 1:
        pad = jnp.concatenate([product] + [nothing] * 3, axis=0)
        inverse_row = inverse_row - mm(roll_lanes(lower, -BLOCK), pad)
    else:
        factor = nothing
    back = tau[m - 1] * prior["off2"][32:64, :] - twice
    back_row = mm(inverse_row, column("back", back))
    left = pick([roll_lanes(inverse_row, -32), roll_lanes(inverse_row, 32), back_row, back_row])
    right = pick([roll_lanes(inverse_row, 32), roll_lanes(inverse_row, -32), roll_lanes(back_row, 32), None])
    done["coef"].append(coef)
    done["inverse"].append(inverse_row)
    done["back"].append(back)
    return dict(
        maps=jnp.concatenate([left, right], axis=1),
        factor=factor,
        upper=roll_lanes(upper, BLOCK * (m - 1)),
        twice=twice,
    )


def mixing_of(t):
    shape = (LANES, LANES)
    lane, row = lanes_of(shape), rows_of(shape)
    out = jnp.zeros(shape, jnp.float32)
    for j in range(1, 5):
        out = jnp.where(row // BLOCK == j - 1, by_block(shape, [t[k][j] for k in range(1, 5)]), out)
    return jnp.where(row % BLOCK == lane % BLOCK, out, 0.0)


def small_outputs(factor, upper, twice, off2, t):
    shape = (LANES, LANES)
    lane, row = lanes_of(shape), rows_of(shape)
    mixing = mixing_of(t)
    triangle = jnp.where(lane >= row, mm(upper + factor.T, mixing), 0.0)
    unit = jnp.where((row // BLOCK == 1) & (row % BLOCK == lane % BLOCK), 1.0, 0.0)
    start = by_block(shape, [t[k][0] for k in range(1, 5)]) * (unit - spread_block(off2, 1))
    projection = exact(twice, mixing, ((0,), (0,))) + start
    return projection, triangle


def eliminate_in(rows_ref):
    def run(work):
        sub = rows_of((8, LANES))
        a = [work[8 * b : 8 * b + 8, :] for b in range(4)]
        for j in range(BLOCK):
            b0, s = divmod(j, 8)
            row = a[b0][s : s + 1, :]
            root = lax.rsqrt(row[:, j : j + 1])
            row = row * root
            rows_ref[j : j + 1, :] = row
            for b in range(b0, 4):
                if b == b0 and s == 7:
                    continue
                column = a[b][:, j : j + 1] * root
                if b == b0:
                    column = jnp.where(sub > s, column, 0.0)
                a[b] = a[b] - column * row
        return rows_ref[...]

    return run


def powers_kernel(
    sizes,
    q_hbm,
    w_hbm,
    shift_ref,
    xa_ref,
    xb_ref,
    maps_ref,
    small_ref,
    q_ref,
    w_ref,
    y_ref,
    field,
    weight,
    coef,
    halo_x,
    halo_y,
    halo_z,
    face_y,
    edge_x,
    edge_y,
    edge_z,
    face_wy,
    rows_ref,
    gathered,
    stream_a,
    stream_2,
    stream_3,
    stream_4,
    load_sem,
    halo_send,
    halo_recv,
    edge_send,
    edge_recv,
    sum_send,
    sum_recv,
):
    nx, ny, nz = sizes
    at = dict(zip(AXES, (lax.axis_index(a) for a in AXES)))
    gx, gy, gz = at["gx"], at["gy"], at["gz"]
    size_of = dict(zip(AXES, sizes))

    def moved(axis, index):
        return tuple(index if a == axis else at[a] for a in AXES)

    def beside(axis, step):
        n = size_of[axis]
        return moved(axis, lax.rem(at[axis] + (n + step), n))

    def partner(axis, d):
        return moved(axis, at[axis] ^ d)

    loads = [
        pltpu.make_async_copy(q_hbm, q_ref, load_sem.at[0]),
        pltpu.make_async_copy(w_hbm, w_ref, load_sem.at[1]),
    ]
    for copy in loads:
        copy.start()

    barrier = pltpu.get_barrier_semaphore()
    peers = 0
    for axis in AXES:
        for d in range(1, size_of[axis]):
            pl.semaphore_signal(barrier, inc=1, device_id=partner(axis, d), device_id_type=MESH)
            peers += 1

    lane = lax.broadcasted_iota(jnp.int32, (16, LANES), 1)
    row = lax.broadcasted_iota(jnp.int32, (16, LANES), 0)
    group = lane // BLOCK

    def q_tile(i, n):
        return q_ref[i, :, n * LANES : (n + 1) * LANES]

    def put(level, i, t, value):
        field[level, i, t] = value
        if level < POWERS:
            face_y[level, 0, 4 * i + t : 4 * i + t + 1, :] = value[15:16, :]
            face_y[level, 1, 4 * i + t : 4 * i + t + 1, :] = value[0:1, :]

    for copy in loads:
        copy.wait()
    for i in range(4):
        for t in range(4):
            put(
                0,
                i,
                t,
                pick([roll_lanes(q_tile(i, 3 * g + V_TILE[t]), BLOCK * g - V_LANE[t]) for g in range(4)]),
            )

    spread_k = lax.broadcasted_iota(jnp.int32, (16, 4 * LANES), 0)
    spread_lane = lax.broadcasted_iota(jnp.int32, (16, 4 * LANES), 1)
    spread = (spread_k == 4 * ((spread_lane % LANES) // BLOCK) + spread_lane // LANES).astype(jnp.float32)
    wide = jnp.dot(
        w_ref[...].reshape(192, 16), spread, precision=lax.Precision.HIGHEST, preferred_element_type=jnp.float32
    )
    for d in range(3):
        for i in range(4):
            for t in range(4):
                r = 16 * (4 * d + i)
                value = wide[r : r + 16, t * LANES : (t + 1) * LANES] * (1.0 / WIDTH)
                weight[d, i, t] = value
                if d == 1:
                    face_wy[4 * i + t : 4 * i + t + 1, :] = value[15:16, :]

    pl.semaphore_wait(barrier, peers)

    def halo_copies(level):
        def copy(src, dst, n, device):
            return pltpu.make_async_remote_copy(
                src_ref=src,
                dst_ref=dst,
                send_sem=halo_send.at[level, n],
                recv_sem=halo_recv.at[level, n],
                device_id=device,
                device_id_type=MESH,
            )

        return [
            copy(field.at[level, 3], halo_x.at[level, 0], 0, beside("gx", 1)),
            copy(field.at[level, 0], halo_x.at[level, 1], 1, beside("gx", -1)),
            copy(field.at[level, :, 3], halo_z.at[level, 0], 2, beside("gz", 1)),
            copy(field.at[level, :, 0], halo_z.at[level, 1], 3, beside("gz", -1)),
            copy(face_y.at[level, 0], halo_y.at[level, 0], 4, beside("gy", 1)),
            copy(face_y.at[level, 1], halo_y.at[level, 1], 5, beside("gy", -1)),
        ]

    def edge_copy(src, dst, n, axis):
        return pltpu.make_async_remote_copy(
            src_ref=src,
            dst_ref=dst,
            send_sem=edge_send.at[n],
            recv_sem=edge_recv.at[n],
            device_id=beside(axis, 1),
            device_id_type=MESH,
        )

    edges = [
        edge_copy(weight.at[0, 3], edge_x, 0, "gx"),
        edge_copy(weight.at[2, :, 3], edge_z, 1, "gz"),
        edge_copy(face_wy, edge_y, 2, "gy"),
    ]
    rounds = [halo_copies(level) for level in range(POWERS)]
    for copy in edges + rounds[0]:
        copy.start()

    for i in range(4):
        rows = slice(16 * i, 16 * i + 16)
        for g in range(4):
            a, b, c = (q_tile(i, 3 * g + n) for n in range(3))
            pairs = [
                roll_lanes(a, 64),
                roll_lanes(jnp.where(lane >= 96, a, b), 96),
                b,
                roll_lanes(c, 32),
            ]
            for t in range(4):
                y_ref[4 * g + t, rows, :] = pairs[t]
                xb_ref[4 * g + t, rows, :] = roll_lanes(field[0, i, t], BLOCK * (2 - g))

    for copy in edges:
        copy.wait_recv()
    low_x, high_x = gx > 0, gx < nx - 1
    low_y, high_y = gy > 0, gy < ny - 1
    low_z, high_z = gz > 0, gz < nz - 1

    def kept(flag):
        return jnp.where(flag, 1.0, 0.0).astype(jnp.float32)

    for i in range(4):
        for t in range(4):
            xp, yp, zp = weight[0, i, t], weight[1, i, t], weight[2, i, t]
            xm = weight[0, i - 1, t] if i > 0 else edge_x[t] * kept(low_x)
            ym = jnp.where(
                row == 0, edge_y[4 * i + t : 4 * i + t + 1, :] * kept(low_y), pltpu.roll(yp, 1, axis=0)
            )
            if t > 0:
                zm = weight[2, i, t - 1]
            else:
                zm = jnp.where(
                    group == 0, roll_lanes(edge_z[i], 32) * kept(low_z), roll_lanes(weight[2, i, 3], 32)
                )
            coef[0, i, t] = ((xp + xm) + (yp + ym)) + (zp + zm) - CENTRE / WIDTH
            coef[1, i, t] = xp * kept(high_x) if i == 3 else xp
            coef[2, i, t] = xm
            coef[3, i, t] = jnp.where(row == 15, yp * kept(high_y), yp)
            coef[4, i, t] = ym
            coef[5, i, t] = jnp.where(group == 3, zp * kept(high_z), zp) if t == 3 else zp
            coef[6, i, t] = zm

    def apply_operator(level):
        for copy in rounds[level]:
            copy.wait_recv()
        for i in range(4):
            for t in range(4):
                centre = field[level, i, t]
                xp = field[level, i + 1, t] if i < 3 else halo_x[level, 1, t]
                xm = field[level, i - 1, t] if i > 0 else halo_x[level, 0, t]
                r = 4 * i + t
                yp = jnp.where(row == 15, halo_y[level, 1, r : r + 1, :], pltpu.roll(centre, 15, axis=0))
                ym = jnp.where(row == 0, halo_y[level, 0, r : r + 1, :], pltpu.roll(centre, 1, axis=0))
                if t < 3:
                    zp = field[level, i, t + 1]
                else:
                    zp = roll_lanes(jnp.where(group == 0, halo_z[level, 1, i], field[level, i, 0]), 96)
                if t > 0:
                    zm = field[level, i, t - 1]
                else:
                    zm = roll_lanes(jnp.where(group == 3, halo_z[level, 0, i], field[level, i, 3]), 32)
                value = coef[0, i, t] * centre
                value = value - (coef[1, i, t] * xp + coef[2, i, t] * xm)
                value = value - (coef[3, i, t] * yp + coef[4, i, t] * ym)
                value = value - (coef[5, i, t] * zp + coef[6, i, t] * zm)
                if level > 0:
                    value = value - field[level - 1, i, t]
                put(level + 1, i, t, value)
        if level + 1 < POWERS:
            for copy in rounds[level + 1]:
                copy.start()

    def products(m):
        for i in range(4):
            for g in range(4):
                for t in range(4):
                    k = 4 * g + t
                    rows = slice(16 * i, 16 * i + 16)
                    y = jnp.where(
                        group == 0,
                        roll_lanes(field[m, i, t], -BLOCK * g),
                        jnp.where(group == 1, roll_lanes(field[m - 1, i, t], BLOCK * (1 - g)), y_ref[k, rows, :]),
                    )
                    y_ref[k, rows, :] = y
                    if m == 2:
                        xa_ref[k, rows, :] = y
                    if m == 4:
                        xb_ref[k, rows, :] = jnp.where(lane < 64, y, xb_ref[k, rows, :])
        y = y_ref[...].reshape(1024, LANES)
        return lax.dot_general(
            y if m == 1 else y[:, :BLOCK],
            y,
            (((0,), (0,)), ((), ())),
            precision=lax.Precision.HIGH,
            preferred_element_type=jnp.float32,
        )

    class Stream:
        def __init__(self, n, rows, refs):
            self.n, self.chunk = n, rows // nx
            self.local, self.part_x, self.part_z, self.part_y, self.total = (
                refs.at[pl.ds(8 * q, 8)] for q in range(5)
            )
            self.whole = refs.at[40]

        def copy(self, src, dst, phase, device):
            return pltpu.make_async_remote_copy(
                src_ref=src,
                dst_ref=dst,
                send_sem=sum_send.at[self.n, phase],
                recv_sem=sum_recv.at[self.n, phase],
                device_id=device,
                device_id_type=MESH,
            )

        def all_of(self, ref, phase):
            axis = ("gx", "gz", "gy", "gx")[phase]
            part = ref.at[pl.ds(1, size_of[axis] - 1)]
            return self.copy(part, part, phase, partner(axis, 1))

        def begin(self, values):
            for c in range(nx):
                self.local[c] = values[c * self.chunk : (c + 1) * self.chunk, :]
            for d in range(1, nx):
                self.copy(self.local.at[gx ^ d], self.part_x.at[d], 0, partner("gx", d)).start()
            self.part_x[0] = self.local[gx]

        def over_z(self):
            self.all_of(self.part_x, 0).wait_recv()
            self.part_z[0] = tree_sum([self.part_x[d] for d in range(nx)])
            for d in range(1, nz):
                self.copy(self.part_z.at[0], self.part_z.at[d], 1, partner("gz", d)).start()

        def over_y(self):
            self.all_of(self.part_z, 1).wait_recv()
            self.part_y[0] = tree_sum([self.part_z[d] for d in range(nz)])
            for d in range(1, ny):
                self.copy(self.part_y.at[0], self.part_y.at[d], 2, partner("gy", d)).start()

        def gather(self):
            self.all_of(self.part_y, 2).wait_recv()
            self.whole[...] = tree_sum([self.part_y[d] for d in range(ny)])
            for d in range(1, nx):
                self.copy(self.whole, self.total.at[gx], 3, partner("gx", d)).start()
            self.total[gx] = self.whole[...]

        def result(self):
            self.all_of(self.total, 3).wait_recv()
            for c in range(nx):
                gathered[c * self.chunk : (c + 1) * self.chunk, :] = self.total[c]
            return gathered[0 : nx * self.chunk, :] * (1.0 / (1024 * nx * ny * nz))

        def drain(self):
            for phase, ref in enumerate((self.part_x, self.part_z, self.part_y, self.total)):
                self.all_of(ref, phase).wait_send()

    a = Stream(0, LANES, stream_a)
    s2, s3, s4 = (Stream(n, BLOCK, ref) for n, ref in ((1, stream_2), (2, stream_3), (3, stream_4)))

    t, tau = scalars(shift_ref[0])
    done = dict(coef=[], inverse=[], back=[])
    known = {}
    eliminate = eliminate_in(rows_ref)

    def block(m, values, prior):
        out = level_algebra(m, values, known, done, prior, tau, eliminate)
        rows = slice(BLOCK * (m - 1), BLOCK * m)
        maps_ref[rows, :] = out["maps"]
        small_ref[0, rows, :] = out["factor"]
        small_ref[1, rows, :] = out["upper"]
        small_ref[2, rows, :] = out["twice"]

    apply_operator(0)
    a.begin(products(1))
    apply_operator(1)
    a.over_z()
    s2.begin(products(2))
    apply_operator(2)
    a.over_y()
    s2.over_z()
    s3.begin(products(3))
    apply_operator(3)
    a.gather()
    s4.begin(products(4))
    s2.over_y()
    s3.over_z()
    s4.over_z()
    gram = a.result()
    known[0] = (gram[32:64, :], 1)
    prior = prior_algebra(gram, tau)
    small_ref[3] = prior["off2"]
    s2.gather()
    s3.over_y()
    block(1, gram[:BLOCK, :], prior)
    s4.over_y()
    s3.gather()
    block(2, s2.result(), prior)
    s4.gather()
    block(3, s3.result(), prior)
    block(4, s4.result(), prior)

    for copy in edges + [c for r in rounds for c in r]:
        copy.wait_send()
    for stream in (a, s2, s3, s4):
        stream.drain()


def basis_kernel(xa_ref, xb_ref, maps_ref, small_ref, shift_ref, new_ref, projection_ref, triangle_ref):
    maps = maps_ref[...]
    for k in range(16):
        both = jnp.concatenate([xa_ref[k], xb_ref[k]], axis=1)
        out = lax.dot_general(
            both,
            maps,
            (((1,), (1,)), ((), ())),
            precision=lax.Precision.HIGH,
            preferred_element_type=jnp.float32,
        )
        for i in range(4):
            new_ref[i, :, k * LANES : (k + 1) * LANES] = out[16 * i : 16 * i + 16, :]
    t, _ = scalars(shift_ref[0])
    projection, triangle = small_outputs(small_ref[0], small_ref[1], small_ref[2], small_ref[3], t)
    projection_ref[0:64, :] = projection[64:, :]
    projection_ref[64:96, :] = projection[32:64, :]
    triangle_ref[...] = triangle


def per_device(sizes, prior_basis, edge_weights, spectral_shift):
    nx, ny, nz = sizes
    f32 = jnp.float32
    tile = (4, 16, LANES)
    vmem = pl.BlockSpec(memory_space=pltpu.VMEM)
    smem = pl.BlockSpec(memory_space=pltpu.SMEM)
    hbm = pl.BlockSpec(memory_space=pltpu.HBM)
    xa, xb, maps, small = pl.pallas_call(
        functools.partial(powers_kernel, sizes),
        out_shape=(
            jax.ShapeDtypeStruct((16, 64, LANES), f32),
            jax.ShapeDtypeStruct((16, 64, LANES), f32),
            jax.ShapeDtypeStruct((LANES, 2 * LANES), f32),
            jax.ShapeDtypeStruct((4, LANES, LANES), f32),
        ),
        in_specs=[hbm, hbm, smem],
        out_specs=(vmem,) * 4,
        scratch_shapes=[
            pltpu.VMEM((4, 16, 16 * BASIS), f32),
            pltpu.VMEM((3, 4, 16, 16), f32),
            pltpu.VMEM((16, 64, LANES), f32),
            pltpu.VMEM((POWERS + 1, 4, *tile), f32),
            pltpu.VMEM((3, 4, *tile), f32),
            pltpu.VMEM((7, 4, *tile), f32),
            pltpu.VMEM((POWERS, 2, *tile), f32),
            pltpu.VMEM((POWERS, 2, 16, LANES), f32),
            pltpu.VMEM((POWERS, 2, *tile), f32),
            pltpu.VMEM((POWERS, 2, 16, LANES), f32),
            pltpu.VMEM(tile, f32),
            pltpu.VMEM((16, LANES), f32),
            pltpu.VMEM(tile, f32),
            pltpu.VMEM((16, LANES), f32),
            pltpu.VMEM((BLOCK, LANES), f32),
            pltpu.VMEM((LANES, LANES), f32),
            pltpu.VMEM((41, LANES // nx, LANES), f32),
            pltpu.VMEM((41, BLOCK // nx, LANES), f32),
            pltpu.VMEM((41, BLOCK // nx, LANES), f32),
            pltpu.VMEM((41, BLOCK // nx, LANES), f32),
            pltpu.SemaphoreType.DMA((2,)),
            pltpu.SemaphoreType.DMA((POWERS, 6)),
            pltpu.SemaphoreType.DMA((POWERS, 6)),
            pltpu.SemaphoreType.DMA((3,)),
            pltpu.SemaphoreType.DMA((3,)),
            pltpu.SemaphoreType.DMA((4, 4)),
            pltpu.SemaphoreType.DMA((4, 4)),
        ],
        name="powers",
        compiler_params=pltpu.CompilerParams(
            collective_id=0, has_side_effects=True, vmem_limit_bytes=40 * 2**20
        ),
    )(prior_basis, edge_weights, spectral_shift)
    return pl.pallas_call(
        basis_kernel,
        out_shape=(
            jax.ShapeDtypeStruct((4, 16, 16 * LANES), f32),
            jax.ShapeDtypeStruct((BASIS, LANES), f32),
            jax.ShapeDtypeStruct((LANES, LANES), f32),
        ),
        in_specs=[vmem, vmem, vmem, vmem, smem],
        out_specs=(vmem, vmem, vmem),
        name="basis",
        compiler_params=pltpu.CompilerParams(vmem_limit_bytes=32 * 2**20),
    )(xa, xb, maps, small, spectral_shift)


def solution(mesh):
    sizes = tuple(mesh.shape[a] for a in AXES)
    return jax.shard_map(
        functools.partial(per_device, sizes),
        mesh=mesh,
        in_specs=(P("gx", "gy", "gz"), P(None, "gx", "gy", "gz"), P()),
        out_specs=(P("gx", "gy", "gz"), P(), P()),
        check_vma=False,
    )
```

```python
import functools
import jax
import jax.numpy as jnp
from jax import lax
from jax.experimental import pallas as pl
from jax.experimental.pallas import tpu as pltpu
from jax.sharding import PartitionSpec as P

BLOCK = 32
POWERS = 4
BASIS = 96
LANES = 128
OPERATOR_SCALE = 11.0
CENTRE = 6.0
WIDTH = 2.5
MESH = pl.DeviceIdType.MESH
AXES = ("gx", "gy", "gz")
V_LANE = (64, 32, 0, 96)
V_TILE = (0, 1, 2, 2)


def roll_lanes(values, shift):
    return values if shift % LANES == 0 else pltpu.roll(values, shift % LANES, axis=values.ndim - 1)


def tree_sum(parts):
    while len(parts) > 1:
        parts = [parts[i] + parts[i + 1] for i in range(0, len(parts), 2)]
    return parts[0]


def exact(a, b, dims):
    return lax.dot_general(
        a, b, (dims, ((), ())), precision=lax.Precision.HIGHEST, preferred_element_type=jnp.float32
    )


def mm(a, b):
    return exact(a, b, ((1,), (0,)))


def mm_t(a, b):
    return exact(a, b, ((1,), (1,)))


def lanes_of(shape):
    return lax.broadcasted_iota(jnp.int32, shape, 1)


def rows_of(shape):
    return lax.broadcasted_iota(jnp.int32, shape, 0)


def by_block(shape, values, dim=1):
    which = lax.broadcasted_iota(jnp.int32, shape, dim) // BLOCK
    out = jnp.full(shape, values[0], jnp.float32)
    for n in range(1, 4):
        out = jnp.where(which == n, values[n], out)
    return out


def pick(parts):
    shape = next(p.shape for p in parts if p is not None)
    which = lanes_of(shape) // BLOCK
    out = jnp.zeros(shape, jnp.float32)
    for n, p in enumerate(parts):
        if p is not None:
            out = jnp.where(which == n, p, out)
    return out


def spread_block(values, block):
    own = jnp.where(lanes_of(values.shape) // BLOCK == block, values, 0.0)
    own = own + roll_lanes(own, 32)
    return own + roll_lanes(own, 64)


def scalars(shift):
    alpha = WIDTH / OPERATOR_SCALE
    beta = (shift + CENTRE) / OPERATOR_SCALE - 1.0
    t = [[1.0, 0.0, 0.0, 0.0, 0.0], [beta, alpha, 0.0, 0.0, 0.0]]
    for k in range(1, POWERS):
        p, before = t[k], t[k - 1]
        row = []
        for j in range(5):
            if j > k + 1:
                row.append(0.0)
                continue
            shifted = (p[j - 1] if j > 0 else 0.0) + (p[j + 1] if j < 4 else 0.0)
            row.append(2.0 * (alpha * shifted + beta * p[j]) - before[j])
        t.append(row)
    tau = []
    for k in range(1, POWERS + 1):
        rest = t[k][0]
        for j in range(1, k):
            rest = rest - t[k][j] * tau[j - 1]
        tau.append(rest * (1.0 / (alpha * (2.0 * alpha) ** (k - 1))))
    return t, tau


def prior_algebra(gram, tau):
    shape = (LANES, LANES)
    lane, row = lanes_of(shape), rows_of(shape)
    inside = (lane >= BLOCK) & (row >= BLOCK)
    prior = jnp.where(inside, gram, 0.0)
    unit = jnp.where(inside & (lane == row), 1.0, 0.0)
    off = unit - prior
    off2 = mm(off, off)
    high = mm(off2, jnp.concatenate([off, off2], axis=1))
    off3, off4 = high[:, :LANES], high[:, LANES:]
    series = (unit + off) + (off2 + off3)
    tau_row = by_block((1, LANES), tau)
    right = jnp.concatenate([series, spread_block(off4, 1) * tau_row, unit + off], axis=1)
    over = off4[32:64, :]
    over_v = mm(over, spread_block(prior, 1) * tau_row)
    return dict(right=right, over=over, over_v=over_v, off2=off2)


def level_algebra(m, products, p, done, prior, tau, eliminate):
    strip = (BLOCK, LANES)
    lane, row = lanes_of(strip), rows_of(strip)
    p[2 * m] = (products, 0)
    p[2 * m - 1] = (products, 1)

    def at(n, block):
        values, own = p[n]
        return roll_lanes(values, BLOCK * (block - own))

    moment = at(m, 1) - at(m - 2, 1) if m > 1 else at(1, 1)
    coef = pick([None, moment, products, products])
    mixed = mm(coef, prior["right"])
    series, over, twice = mixed[:, :LANES], mixed[:, LANES : 2 * LANES], mixed[:, 2 * LANES :]
    blocks = [None] * 4
    for k in range(1, m + 1):
        value = at(m + k, k - 1)
        if m - k >= 2:
            value = value - at(m - k - 2, k - 1)
        blocks[k - 1] = value
    nothing = jnp.zeros(strip, jnp.float32)

    def column(name, own):
        parts = done[name] + [own]
        return jnp.concatenate(parts + [nothing] * (4 - len(parts)), axis=0)

    coefs = column("coef", coef)
    inverse = column("inverse", nothing)
    gram = pick(blocks) + over + tau[m - 1] * prior["over_v"]
    gram = gram + mm_t(tau[m - 1] * prior["over"] - series, coefs)
    below = roll_lanes(gram, -BLOCK * (m - 1))
    if m > 1:
        factor = mm_t(gram, inverse)
        pad = jnp.concatenate([factor] + [nothing] * 3, axis=0)
        below = below - mm_t(factor, pad)
        product = mm(factor, inverse)
    work = jnp.where(lane < BLOCK, below, jnp.where(lane == row + BLOCK, 1.0, 0.0))
    work = eliminate(work)
    upper = jnp.where((lane < BLOCK) & (lane >= row), work, 0.0)
    lower = jnp.where((lane >= BLOCK) & (lane <= row + BLOCK), work, 0.0)
    inverse_row = roll_lanes(lower, BLOCK * (m - 2))
    if m > 1:
        pad = jnp.concatenate([product] + [nothing] * 3, axis=0)
        inverse_row = inverse_row - mm(roll_lanes(lower, -BLOCK), pad)
    else:
        factor = nothing
    back = tau[m - 1] * prior["off2"][32:64, :] - twice
    back_row = mm(inverse_row, column("back", back))
    left = pick([roll_lanes(inverse_row, -32), roll_lanes(inverse_row, 32), back_row, back_row])
    right = pick([roll_lanes(inverse_row, 32), roll_lanes(inverse_row, -32), roll_lanes(back_row, 32), None])
    done["coef"].append(coef)
    done["inverse"].append(inverse_row)
    done["back"].append(back)
    return dict(
        maps=jnp.concatenate([left, right], axis=1),
        factor=factor,
        upper=roll_lanes(upper, BLOCK * (m - 1)),
        twice=twice,
    )


def mixing_of(t):
    shape = (LANES, LANES)
    lane, row = lanes_of(shape), rows_of(shape)
    out = jnp.zeros(shape, jnp.float32)
    for j in range(1, 5):
        out = jnp.where(row // BLOCK == j - 1, by_block(shape, [t[k][j] for k in range(1, 5)]), out)
    return jnp.where(row % BLOCK == lane % BLOCK, out, 0.0)


def small_outputs(factor, upper, twice, off2, t):
    shape = (LANES, LANES)
    lane, row = lanes_of(shape), rows_of(shape)
    mixing = mixing_of(t)
    triangle = jnp.where(lane >= row, mm(upper + factor.T, mixing), 0.0)
    unit = jnp.where((row // BLOCK == 1) & (row % BLOCK == lane % BLOCK), 1.0, 0.0)
    start = by_block(shape, [t[k][0] for k in range(1, 5)]) * (unit - spread_block(off2, 1))
    projection = exact(twice, mixing, ((0,), (0,))) + start
    return projection, triangle


def eliminate_in(rows_ref):
    def run(work):
        sub = rows_of((8, LANES))
        a = [work[8 * b : 8 * b + 8, :] for b in range(4)]
        for b0 in range(4):
            columns = [
                [jnp.broadcast_to(a[b][:, 8 * b0 + n : 8 * b0 + n + 1], (8, LANES)) for b in range(b0, 4)]
                for n in range(8)
            ]
            for s in range(8):
                root = lax.rsqrt(columns[s][0][s : s + 1, :])
                row = a[b0][s : s + 1, :] * root
                rows_ref[8 * b0 + s : 8 * b0 + s + 1, :] = row
                scaled = [c * root for c in columns[s]]
                scaled[0] = jnp.where(sub > s, scaled[0], 0.0)
                for n in range(s + 1, 8):
                    weight = columns[n][0][s : s + 1, :] * root
                    columns[n] = [c - m * weight for c, m in zip(columns[n], scaled)]
                for b in range(b0, 4):
                    a[b] = a[b] - scaled[b - b0] * row
        return rows_ref[...]

    return run


def powers_kernel(
    sizes,
    q_hbm,
    w_hbm,
    shift_ref,
    xa_ref,
    xb_ref,
    maps_ref,
    small_ref,
    q_ref,
    w_ref,
    y_ref,
    field,
    weight,
    coef,
    rim_x,
    rim_y,
    rim_z,
    halo_x,
    halo_y,
    halo_z,
    face_y,
    edge_x,
    edge_y,
    edge_z,
    face_wy,
    rows_ref,
    gathered,
    stream_a,
    stream_2,
    stream_3,
    stream_4,
    load_sem,
    halo_send,
    halo_recv,
    edge_send,
    edge_recv,
    sum_send,
    sum_recv,
):
    nx, ny, nz = sizes
    at = dict(zip(AXES, (lax.axis_index(a) for a in AXES)))
    gx, gy, gz = at["gx"], at["gy"], at["gz"]
    size_of = dict(zip(AXES, sizes))

    def moved(axis, index):
        return tuple(index if a == axis else at[a] for a in AXES)

    def beside(axis, step):
        n = size_of[axis]
        return moved(axis, lax.rem(at[axis] + (n + step), n))

    def partner(axis, d):
        return moved(axis, at[axis] ^ d)

    loads = [
        pltpu.make_async_copy(q_hbm, q_ref, load_sem.at[0]),
        pltpu.make_async_copy(w_hbm, w_ref, load_sem.at[1]),
    ]
    for copy in loads:
        copy.start()

    barrier = pltpu.get_barrier_semaphore()
    peers = 0
    for d in range(max(sizes) - 1, 0, -1):
        for axis in ("gy", "gz", "gx"):
            if d < size_of[axis]:
                pl.semaphore_signal(barrier, inc=1, device_id=partner(axis, d), device_id_type=MESH)
                peers += 1

    lane = lax.broadcasted_iota(jnp.int32, (16, LANES), 1)
    row = lax.broadcasted_iota(jnp.int32, (16, LANES), 0)
    group = lane // BLOCK

    def q_tile(i, n):
        return q_ref[i, :, n * LANES : (n + 1) * LANES]

    def put(level, i, t, value):
        field[level, i, t] = value
        if level < POWERS:
            face_y[level, 0, 4 * i + t : 4 * i + t + 1, :] = value[15:16, :]
            face_y[level, 1, 4 * i + t : 4 * i + t + 1, :] = value[0:1, :]

    for copy in loads:
        copy.wait()
    for i in range(4):
        for t in range(4):
            put(
                0,
                i,
                t,
                pick([roll_lanes(q_tile(i, 3 * g + V_TILE[t]), BLOCK * g - V_LANE[t]) for g in range(4)]),
            )

    spread_k = lax.broadcasted_iota(jnp.int32, (16, 4 * LANES), 0)
    spread_lane = lax.broadcasted_iota(jnp.int32, (16, 4 * LANES), 1)
    spread = (spread_k == 4 * ((spread_lane % LANES) // BLOCK) + spread_lane // LANES).astype(jnp.float32)
    wide = jnp.dot(
        w_ref[...].reshape(192, 16), spread, precision=lax.Precision.HIGHEST, preferred_element_type=jnp.float32
    )
    for d in range(3):
        for i in range(4):
            for t in range(4):
                r = 16 * (4 * d + i)
                value = wide[r : r + 16, t * LANES : (t + 1) * LANES] * (1.0 / WIDTH)
                weight[d, i, t] = value
                if d == 1:
                    face_wy[4 * i + t : 4 * i + t + 1, :] = value[15:16, :]

    pl.semaphore_wait(barrier, peers)

    def halo_copies(level):
        def copy(src, dst, n, device):
            return pltpu.make_async_remote_copy(
                src_ref=src,
                dst_ref=dst,
                send_sem=halo_send.at[level, n],
                recv_sem=halo_recv.at[level, n],
                device_id=device,
                device_id_type=MESH,
            )

        return [
            copy(field.at[level, 3], halo_x.at[level, 0], 0, beside("gx", 1)),
            copy(field.at[level, 0], halo_x.at[level, 1], 1, beside("gx", -1)),
            copy(field.at[level, :, 3], halo_z.at[level, 0], 2, beside("gz", 1)),
            copy(field.at[level, :, 0], halo_z.at[level, 1], 3, beside("gz", -1)),
            copy(face_y.at[level, 0], halo_y.at[level, 0], 4, beside("gy", 1)),
            copy(face_y.at[level, 1], halo_y.at[level, 1], 5, beside("gy", -1)),
        ]

    def edge_copy(src, dst, n, axis):
        return pltpu.make_async_remote_copy(
            src_ref=src,
            dst_ref=dst,
            send_sem=edge_send.at[n],
            recv_sem=edge_recv.at[n],
            device_id=beside(axis, 1),
            device_id_type=MESH,
        )

    edges = [
        edge_copy(weight.at[0, 3], edge_x, 0, "gx"),
        edge_copy(weight.at[2, :, 3], edge_z, 1, "gz"),
        edge_copy(face_wy, edge_y, 2, "gy"),
    ]
    rounds = [halo_copies(level) for level in range(POWERS)]
    for copy in edges + rounds[0]:
        copy.start()

    for i in range(4):
        rows = slice(16 * i, 16 * i + 16)
        for g in range(4):
            a, b, c = (q_tile(i, 3 * g + n) for n in range(3))
            pairs = [
                roll_lanes(a, 64),
                roll_lanes(jnp.where(lane >= 96, a, b), 96),
                b,
                roll_lanes(c, 32),
            ]
            for t in range(4):
                y_ref[4 * g + t, rows, :] = pairs[t]
                xb_ref[4 * g + t, rows, :] = roll_lanes(field[0, i, t], BLOCK * (2 - g))

    for copy in edges:
        copy.wait_recv()
    low_x, high_x = gx > 0, gx < nx - 1
    low_y, high_y = gy > 0, gy < ny - 1
    low_z, high_z = gz > 0, gz < nz - 1

    def kept(flag):
        return jnp.where(flag, 1.0, 0.0).astype(jnp.float32)

    for i in range(4):
        for t in range(4):
            r = slice(4 * i + t, 4 * i + t + 1)
            xp, yp, zp = weight[0, i, t], weight[1, i, t], weight[2, i, t]
            if i > 0:
                xm = weight[0, i - 1, t]
            else:
                xm = edge_x[t] * kept(low_x)
                rim_x[0, t] = xm
            if i == 3:
                rim_x[1, t] = xp * kept(high_x)
            below = edge_y[r, :] * kept(low_y)
            rim_y[0, r, :] = below
            rim_y[1, r, :] = yp[15:16, :] * kept(high_y)
            ym = pltpu.roll(yp, 1, axis=0)
            ym_all = jnp.where(row == 0, below, ym)
            if t > 0:
                zm = zm_all = weight[2, i, t - 1]
            else:
                rim = jnp.where(group == 0, roll_lanes(edge_z[i], 32) * kept(low_z), 0.0)
                rim_z[0, i] = rim
                zm = jnp.where(group == 0, 0.0, roll_lanes(weight[2, i, 3], 32))
                zm_all = zm + rim
            if t == 3:
                rim_z[1, i] = jnp.where(group == 3, zp * kept(high_z), 0.0)
            coef[0, i, t] = ((xp + xm) + (yp + ym_all)) + (zp + zm_all) - CENTRE / WIDTH
            coef[1, i, t] = xp
            coef[2, i, t] = xm
            coef[3, i, t] = jnp.where(row == 15, 0.0, yp)
            coef[4, i, t] = jnp.where(row == 0, 0.0, ym)
            coef[5, i, t] = jnp.where(group == 3, 0.0, zp) if t == 3 else zp
            coef[6, i, t] = zm

    def apply_inside(level):
        for i in range(4):
            for t in range(4):
                centre = field[level, i, t]
                yp, ym = pltpu.roll(centre, 15, axis=0), pltpu.roll(centre, 1, axis=0)
                zp = field[level, i, t + 1] if t < 3 else roll_lanes(field[level, i, 0], 96)
                zm = field[level, i, t - 1] if t > 0 else roll_lanes(field[level, i, 3], 32)
                value = coef[0, i, t] * centre
                if i < 3:
                    value = value - coef[1, i, t] * field[level, i + 1, t]
                if i > 0:
                    value = value - coef[2, i, t] * field[level, i - 1, t]
                value = value - (coef[3, i, t] * yp + coef[4, i, t] * ym)
                value = value - (coef[5, i, t] * zp + coef[6, i, t] * zm)
                if level > 0:
                    value = value - field[level - 1, i, t]
                field[level + 1, i, t] = value

    def apply_faces(level):
        for copy in rounds[level]:
            copy.wait_recv()
        following = rounds[level + 1] if level + 1 < POWERS else []
        low = rim_y[0] * halo_y[level, 0]
        high = rim_y[1] * halo_y[level, 1]
        for i in (3, 0, 1, 2):
            for t in range(4):
                r = slice(4 * i + t, 4 * i + t + 1)
                value = field[level + 1, i, t]
                if i == 3:
                    value = value - rim_x[1, t] * halo_x[level, 1, t]
                if i == 0:
                    value = value - rim_x[0, t] * halo_x[level, 0, t]
                value = value - jnp.where(row == 0, low[r, :], jnp.where(row == 15, high[r, :], 0.0))
                if t == 3:
                    value = value - rim_z[1, i] * roll_lanes(halo_z[level, 1, i], 96)
                if t == 0:
                    value = value - rim_z[0, i] * roll_lanes(halo_z[level, 0, i], 32)
                put(level + 1, i, t, value)
            if i == 0:
                for copy in following[:2]:
                    copy.start()
        for copy in following[2:]:
            copy.start()

    def prepare(m):
        for i in range(4):
            rows = slice(16 * i, 16 * i + 16)
            for g in range(4):
                for t in range(4):
                    k = 4 * g + t
                    y_ref[k, rows, :] = jnp.where(
                        group == 1, roll_lanes(field[m - 1, i, t], BLOCK * (1 - g)), y_ref[k, rows, :]
                    )

    def products(m):
        for i in range(4):
            rows = slice(16 * i, 16 * i + 16)
            for g in range(4):
                for t in range(4):
                    k = 4 * g + t
                    y_ref[k, rows, :] = jnp.where(group == 0, roll_lanes(field[m, i, t], -BLOCK * g), y_ref[k, rows, :])
        y = y_ref[...].reshape(1024, LANES)
        return lax.dot_general(
            y if m == 1 else y[:, :BLOCK],
            y,
            (((0,), (0,)), ((), ())),
            precision=lax.Precision.HIGH,
            preferred_element_type=jnp.float32,
        )

    class Stream:
        def __init__(self, n, rows, refs):
            self.n, self.chunk = n, rows // nx
            self.local, self.part_x, self.part_z, self.part_y, self.total = (
                refs.at[pl.ds(8 * q, 8)] for q in range(5)
            )
            self.whole = refs.at[40]

        def copy(self, src, dst, phase, device):
            return pltpu.make_async_remote_copy(
                src_ref=src,
                dst_ref=dst,
                send_sem=sum_send.at[self.n, phase],
                recv_sem=sum_recv.at[self.n, phase],
                device_id=device,
                device_id_type=MESH,
            )

        def all_of(self, ref, phase):
            axis = ("gx", "gz", "gy", "gx")[phase]
            part = ref.at[pl.ds(1, size_of[axis] - 1)]
            return self.copy(part, part, phase, partner(axis, 1))

        def begin(self, values):
            for c in range(nx):
                self.local[c] = values[c * self.chunk : (c + 1) * self.chunk, :]
            for d in range(1, nx):
                self.copy(self.local.at[gx ^ d], self.part_x.at[d], 0, partner("gx", d)).start()
            self.part_x[0] = self.local[gx]

        def over_z(self):
            self.all_of(self.part_x, 0).wait_recv()
            self.part_z[0] = tree_sum([self.part_x[d] for d in range(nx)])
            for d in range(1, nz):
                self.copy(self.part_z.at[0], self.part_z.at[d], 1, partner("gz", d)).start()

        def over_y(self):
            self.all_of(self.part_z, 1).wait_recv()
            self.part_y[0] = tree_sum([self.part_z[d] for d in range(nz)])
            for d in range(1, ny):
                self.copy(self.part_y.at[0], self.part_y.at[d], 2, partner("gy", d)).start()

        def gather(self):
            self.all_of(self.part_y, 2).wait_recv()
            self.whole[...] = tree_sum([self.part_y[d] for d in range(ny)])
            for d in range(1, nx):
                self.copy(self.whole, self.total.at[gx], 3, partner("gx", d)).start()
            self.total[gx] = self.whole[...]

        def result(self):
            self.all_of(self.total, 3).wait_recv()
            for c in range(nx):
                gathered[c * self.chunk : (c + 1) * self.chunk, :] = self.total[c]
            return gathered[0 : nx * self.chunk, :] * (1.0 / (1024 * nx * ny * nz))

        def drain(self):
            for phase, ref in enumerate((self.part_x, self.part_z, self.part_y, self.total)):
                self.all_of(ref, phase).wait_send()

    a = Stream(0, LANES, stream_a)
    s2, s3, s4 = (Stream(n, BLOCK, ref) for n, ref in ((1, stream_2), (2, stream_3), (3, stream_4)))

    t, tau = scalars(shift_ref[0])
    done = dict(coef=[], inverse=[], back=[])
    known = {}
    eliminate = eliminate_in(rows_ref)

    def block(m, values, prior):
        out = level_algebra(m, values, known, done, prior, tau, eliminate)
        rows = slice(BLOCK * (m - 1), BLOCK * m)
        maps_ref[rows, :] = out["maps"]
        small_ref[0, rows, :] = out["factor"]
        small_ref[1, rows, :] = out["upper"]
        small_ref[2, rows, :] = out["twice"]

    apply_inside(0)
    prepare(1)
    apply_faces(0)
    apply_inside(1)
    a.begin(products(1))
    prepare(2)
    apply_faces(1)
    apply_inside(2)
    a.over_z()
    s2.begin(products(2))
    xa_ref[...] = y_ref[...]
    prepare(3)
    apply_faces(2)
    apply_inside(3)
    a.over_y()
    s2.over_z()
    s3.begin(products(3))
    prepare(4)
    apply_faces(3)
    s4.begin(products(4))
    a.gather()
    s2.over_y()
    s3.over_z()
    for k in range(16):
        wide_lane = lax.broadcasted_iota(jnp.int32, (64, LANES), 1)
        xb_ref[k] = jnp.where(wide_lane < 64, y_ref[k], xb_ref[k])
    s4.over_z()
    gram = a.result()
    known[0] = (gram[32:64, :], 1)
    prior = prior_algebra(gram, tau)
    small_ref[3] = prior["off2"]
    s2.gather()
    s3.over_y()
    block(1, gram[:BLOCK, :], prior)
    s4.over_y()
    s3.gather()
    block(2, s2.result(), prior)
    s4.gather()
    block(3, s3.result(), prior)
    block(4, s4.result(), prior)

    for copy in edges + [c for r in rounds for c in r]:
        copy.wait_send()
    for stream in (a, s2, s3, s4):
        stream.drain()


def basis_kernel(xa_ref, xb_ref, maps_ref, small_ref, shift_ref, new_ref, projection_ref, triangle_ref):
    maps = maps_ref[...]
    for k in range(16):
        both = jnp.concatenate([xa_ref[k], xb_ref[k]], axis=1)
        out = lax.dot_general(
            both,
            maps,
            (((1,), (1,)), ((), ())),
            precision=lax.Precision.HIGH,
            preferred_element_type=jnp.float32,
        )
        for i in range(4):
            new_ref[i, :, k * LANES : (k + 1) * LANES] = out[16 * i : 16 * i + 16, :]
    t, _ = scalars(shift_ref[0])
    projection, triangle = small_outputs(small_ref[0], small_ref[1], small_ref[2], small_ref[3], t)
    projection_ref[0:64, :] = projection[64:, :]
    projection_ref[64:96, :] = projection[32:64, :]
    triangle_ref[...] = triangle


def per_device(sizes, prior_basis, edge_weights, spectral_shift):
    nx, ny, nz = sizes
    f32 = jnp.float32
    tile = (4, 16, LANES)
    vmem = pl.BlockSpec(memory_space=pltpu.VMEM)
    smem = pl.BlockSpec(memory_space=pltpu.SMEM)
    hbm = pl.BlockSpec(memory_space=pltpu.HBM)
    xa, xb, maps, small = pl.pallas_call(
        functools.partial(powers_kernel, sizes),
        out_shape=(
            jax.ShapeDtypeStruct((16, 64, LANES), f32),
            jax.ShapeDtypeStruct((16, 64, LANES), f32),
            jax.ShapeDtypeStruct((LANES, 2 * LANES), f32),
            jax.ShapeDtypeStruct((4, LANES, LANES), f32),
        ),
        in_specs=[hbm, hbm, smem],
        out_specs=(vmem,) * 4,
        scratch_shapes=[
            pltpu.VMEM((4, 16, 16 * BASIS), f32),
            pltpu.VMEM((3, 4, 16, 16), f32),
            pltpu.VMEM((16, 64, LANES), f32),
            pltpu.VMEM((POWERS + 1, 4, *tile), f32),
            pltpu.VMEM((3, 4, *tile), f32),
            pltpu.VMEM((7, 4, *tile), f32),
            pltpu.VMEM((2, *tile), f32),
            pltpu.VMEM((2, 16, LANES), f32),
            pltpu.VMEM((2, *tile), f32),
            pltpu.VMEM((POWERS, 2, *tile), f32),
            pltpu.VMEM((POWERS, 2, 16, LANES), f32),
            pltpu.VMEM((POWERS, 2, *tile), f32),
            pltpu.VMEM((POWERS, 2, 16, LANES), f32),
            pltpu.VMEM(tile, f32),
            pltpu.VMEM((16, LANES), f32),
            pltpu.VMEM(tile, f32),
            pltpu.VMEM((16, LANES), f32),
            pltpu.VMEM((BLOCK, LANES), f32),
            pltpu.VMEM((LANES, LANES), f32),
            pltpu.VMEM((41, LANES // nx, LANES), f32),
            pltpu.VMEM((41, BLOCK // nx, LANES), f32),
            pltpu.VMEM((41, BLOCK // nx, LANES), f32),
            pltpu.VMEM((41, BLOCK // nx, LANES), f32),
            pltpu.SemaphoreType.DMA((2,)),
            pltpu.SemaphoreType.DMA((POWERS, 6)),
            pltpu.SemaphoreType.DMA((POWERS, 6)),
            pltpu.SemaphoreType.DMA((3,)),
            pltpu.SemaphoreType.DMA((3,)),
            pltpu.SemaphoreType.DMA((4, 4)),
            pltpu.SemaphoreType.DMA((4, 4)),
        ],
        name="powers",
        compiler_params=pltpu.CompilerParams(
            collective_id=0, has_side_effects=True, vmem_limit_bytes=40 * 2**20
        ),
    )(
        pltpu.with_memory_space_constraint(prior_basis, pltpu.HBM),
        pltpu.with_memory_space_constraint(edge_weights, pltpu.HBM),
        spectral_shift,
    )
    return pl.pallas_call(
        basis_kernel,
        out_shape=(
            jax.ShapeDtypeStruct((4, 16, 16 * LANES), f32),
            jax.ShapeDtypeStruct((BASIS, LANES), f32),
            jax.ShapeDtypeStruct((LANES, LANES), f32),
        ),
        in_specs=[vmem, vmem, vmem, vmem, smem],
        out_specs=(vmem, vmem, vmem),
        name="basis",
        compiler_params=pltpu.CompilerParams(vmem_limit_bytes=32 * 2**20),
    )(xa, xb, maps, small, spectral_shift)


def solution(mesh):
    sizes = tuple(mesh.shape[a] for a in AXES)
    return jax.shard_map(
        functools.partial(per_device, sizes),
        mesh=mesh,
        in_specs=(P("gx", "gy", "gz"), P(None, "gx", "gy", "gz"), P()),
        out_specs=(P("gx", "gy", "gz"), P(), P()),
        check_vma=False,
    )
```

```python
import functools
import jax
import jax.numpy as jnp
from jax import lax
from jax.experimental import pallas as pl
from jax.experimental.pallas import tpu as pltpu
from jax.sharding import PartitionSpec as P

BLOCK = 32
POWERS = 4
BASIS = 96
LANES = 128
OPERATOR_SCALE = 11.0
CENTRE = 6.0
WIDTH = 2.5
MESH = pl.DeviceIdType.MESH
AXES = ("gx", "gy", "gz")
V_LANE = (64, 32, 0, 96)
V_TILE = (0, 1, 2, 2)


def roll_lanes(values, shift):
    return values if shift % LANES == 0 else pltpu.roll(values, shift % LANES, axis=values.ndim - 1)


def tree_sum(parts):
    while len(parts) > 1:
        parts = [parts[i] + parts[i + 1] for i in range(0, len(parts), 2)]
    return parts[0]


def exact(a, b, dims):
    return lax.dot_general(
        a, b, (dims, ((), ())), precision=lax.Precision.HIGHEST, preferred_element_type=jnp.float32
    )


def mm(a, b):
    return exact(a, b, ((1,), (0,)))


def mm_t(a, b):
    return exact(a, b, ((1,), (1,)))


def lanes_of(shape):
    return lax.broadcasted_iota(jnp.int32, shape, 1)


def rows_of(shape):
    return lax.broadcasted_iota(jnp.int32, shape, 0)


def by_block(shape, values, dim=1):
    which = lax.broadcasted_iota(jnp.int32, shape, dim) // BLOCK
    out = jnp.full(shape, values[0], jnp.float32)
    for n in range(1, 4):
        out = jnp.where(which == n, values[n], out)
    return out


def pick(parts):
    shape = next(p.shape for p in parts if p is not None)
    which = lanes_of(shape) // BLOCK
    out = jnp.zeros(shape, jnp.float32)
    for n, p in enumerate(parts):
        if p is not None:
            out = jnp.where(which == n, p, out)
    return out


def spread_block(values, block):
    own = jnp.where(lanes_of(values.shape) // BLOCK == block, values, 0.0)
    own = own + roll_lanes(own, 32)
    return own + roll_lanes(own, 64)


def scalars(shift):
    alpha = WIDTH / OPERATOR_SCALE
    beta = (shift + CENTRE) / OPERATOR_SCALE - 1.0
    t = [[1.0, 0.0, 0.0, 0.0, 0.0], [beta, alpha, 0.0, 0.0, 0.0]]
    for k in range(1, POWERS):
        p, before = t[k], t[k - 1]
        row = []
        for j in range(5):
            if j > k + 1:
                row.append(0.0)
                continue
            shifted = (p[j - 1] if j > 0 else 0.0) + (p[j + 1] if j < 4 else 0.0)
            row.append(2.0 * (alpha * shifted + beta * p[j]) - before[j])
        t.append(row)
    tau = []
    for k in range(1, POWERS + 1):
        rest = t[k][0]
        for j in range(1, k):
            rest = rest - t[k][j] * tau[j - 1]
        tau.append(rest * (1.0 / (alpha * (2.0 * alpha) ** (k - 1))))
    return t, tau


def prior_algebra(gram, tau):
    shape = (LANES, LANES)
    lane, row = lanes_of(shape), rows_of(shape)
    inside = (lane >= BLOCK) & (row >= BLOCK)
    prior = jnp.where(inside, gram, 0.0)
    unit = jnp.where(inside & (lane == row), 1.0, 0.0)
    off = unit - prior
    off2 = mm(off, off)
    high = mm(off2, jnp.concatenate([off, off2], axis=1))
    off3, off4 = high[:, :LANES], high[:, LANES:]
    series = (unit + off) + (off2 + off3)
    tau_row = by_block((1, LANES), tau)
    right = jnp.concatenate([series, spread_block(off4, 1) * tau_row, unit + off], axis=1)
    over = off4[32:64, :]
    over_v = mm(over, spread_block(prior, 1) * tau_row)
    return dict(right=right, over=over, over_v=over_v, off2=off2)


def level_algebra(m, products, p, done, prior, tau, eliminate):
    strip = (BLOCK, LANES)
    lane, row = lanes_of(strip), rows_of(strip)
    p[2 * m] = (products, 0)
    p[2 * m - 1] = (products, 1)

    def at(n, block):
        values, own = p[n]
        return roll_lanes(values, BLOCK * (block - own))

    moment = at(m, 1) - at(m - 2, 1) if m > 1 else at(1, 1)
    coef = pick([None, moment, products, products])
    mixed = mm(coef, prior["right"])
    series, over, twice = mixed[:, :LANES], mixed[:, LANES : 2 * LANES], mixed[:, 2 * LANES :]
    blocks = [None] * 4
    for k in range(1, m + 1):
        value = at(m + k, k - 1)
        if m - k >= 2:
            value = value - at(m - k - 2, k - 1)
        blocks[k - 1] = value
    nothing = jnp.zeros(strip, jnp.float32)

    def column(name, own):
        parts = done[name] + [own]
        return jnp.concatenate(parts + [nothing] * (4 - len(parts)), axis=0)

    coefs = column("coef", coef)
    inverse = column("inverse", nothing)
    gram = pick(blocks) + over + tau[m - 1] * prior["over_v"]
    gram = gram + mm_t(tau[m - 1] * prior["over"] - series, coefs)
    below = roll_lanes(gram, -BLOCK * (m - 1))
    if m > 1:
        factor = mm_t(gram, inverse)
        pad = jnp.concatenate([factor] + [nothing] * 3, axis=0)
        below = below - mm_t(factor, pad)
        product = mm(factor, inverse)
    work = jnp.where(lane < BLOCK, below, jnp.where(lane == row + BLOCK, 1.0, 0.0))
    work = eliminate(work)
    upper = jnp.where((lane < BLOCK) & (lane >= row), work, 0.0)
    lower = jnp.where((lane >= BLOCK) & (lane <= row + BLOCK), work, 0.0)
    inverse_row = roll_lanes(lower, BLOCK * (m - 2))
    if m > 1:
        pad = jnp.concatenate([product] + [nothing] * 3, axis=0)
        inverse_row = inverse_row - mm(roll_lanes(lower, -BLOCK), pad)
    else:
        factor = nothing
    back = tau[m - 1] * prior["off2"][32:64, :] - twice
    back_row = mm(inverse_row, column("back", back))
    left = pick([roll_lanes(inverse_row, -32), roll_lanes(inverse_row, 32), back_row, back_row])
    right = pick([roll_lanes(inverse_row, 32), roll_lanes(inverse_row, -32), roll_lanes(back_row, 32), None])
    done["coef"].append(coef)
    done["inverse"].append(inverse_row)
    done["back"].append(back)
    return dict(
        maps=jnp.concatenate([left, right], axis=1),
        factor=factor,
        upper=roll_lanes(upper, BLOCK * (m - 1)),
        twice=twice,
    )


def mixing_of(t):
    shape = (LANES, LANES)
    lane, row = lanes_of(shape), rows_of(shape)
    out = jnp.zeros(shape, jnp.float32)
    for j in range(1, 5):
        out = jnp.where(row // BLOCK == j - 1, by_block(shape, [t[k][j] for k in range(1, 5)]), out)
    return jnp.where(row % BLOCK == lane % BLOCK, out, 0.0)


def small_outputs(factor, upper, twice, off2, t):
    shape = (LANES, LANES)
    lane, row = lanes_of(shape), rows_of(shape)
    mixing = mixing_of(t)
    triangle = jnp.where(lane >= row, mm(upper + factor.T, mixing), 0.0)
    unit = jnp.where((row // BLOCK == 1) & (row % BLOCK == lane % BLOCK), 1.0, 0.0)
    start = by_block(shape, [t[k][0] for k in range(1, 5)]) * (unit - spread_block(off2, 1))
    projection = exact(twice, mixing, ((0,), (0,))) + start
    return projection, triangle


def eliminate_in(rows_ref):
    def run(work):
        sub = rows_of((8, LANES))
        a = [work[8 * b : 8 * b + 8, :] for b in range(4)]
        for b0 in range(4):
            columns = [
                [jnp.broadcast_to(a[b][:, 8 * b0 + n : 8 * b0 + n + 1], (8, LANES)) for b in range(b0, 4)]
                for n in range(8)
            ]
            for s in range(8):
                root = lax.rsqrt(columns[s][0][s : s + 1, :])
                row = a[b0][s : s + 1, :] * root
                rows_ref[8 * b0 + s : 8 * b0 + s + 1, :] = row
                scaled = [c * root for c in columns[s]]
                scaled[0] = jnp.where(sub > s, scaled[0], 0.0)
                for n in range(s + 1, 8):
                    weight = columns[n][0][s : s + 1, :] * root
                    columns[n] = [c - m * weight for c, m in zip(columns[n], scaled)]
                for b in range(b0, 4):
                    a[b] = a[b] - scaled[b - b0] * row
        return rows_ref[...]

    return run


def powers_kernel(
    sizes,
    q_hbm,
    w_hbm,
    shift_ref,
    xa_ref,
    xb_ref,
    maps_ref,
    small_ref,
    q_ref,
    w_ref,
    y_ref,
    field,
    weight,
    coef,
    rim_x,
    rim_y,
    rim_z,
    halo_x,
    halo_y,
    halo_z,
    face_y,
    face_z,
    edge_x,
    edge_y,
    edge_z,
    face_wy,
    rows_ref,
    gathered,
    stream_a,
    stream_2,
    stream_3,
    stream_4,
    load_sem,
    halo_send,
    halo_recv,
    edge_send,
    edge_recv,
    sum_send,
    sum_recv,
    ready_sem,
):
    nx, ny, nz = sizes
    at = dict(zip(AXES, (lax.axis_index(a) for a in AXES)))
    gx, gy, gz = at["gx"], at["gy"], at["gz"]
    size_of = dict(zip(AXES, sizes))

    def moved(axis, index):
        return tuple(index if a == axis else at[a] for a in AXES)

    def beside(axis, step):
        n = size_of[axis]
        return moved(axis, lax.rem(at[axis] + (n + step), n))

    def partner(axis, d):
        return moved(axis, at[axis] ^ d)

    loads = [
        pltpu.make_async_copy(q_hbm, q_ref, load_sem.at[0]),
        pltpu.make_async_copy(w_hbm, w_ref, load_sem.at[1]),
    ]
    for copy in loads:
        copy.start()

    barrier = pltpu.get_barrier_semaphore()
    for axis in AXES:
        for step in (1, -1):
            pl.semaphore_signal(barrier, inc=1, device_id=beside(axis, step), device_id_type=MESH)

    lane = lax.broadcasted_iota(jnp.int32, (16, LANES), 1)
    row = lax.broadcasted_iota(jnp.int32, (16, LANES), 0)
    group = lane // BLOCK

    def q_tile(i, n):
        return q_ref[i, :, n * LANES : (n + 1) * LANES]

    def put(level, i, t, value):
        field[level, i, t] = value
        if level < POWERS:
            face_y[level, 0, 4 * i + t : 4 * i + t + 1, :] = value[15:16, :]
            face_y[level, 1, 4 * i + t : 4 * i + t + 1, :] = value[0:1, :]

    for copy in loads:
        copy.wait()
    for i in range(4):
        for t in range(4):
            put(
                0,
                i,
                t,
                pick([roll_lanes(q_tile(i, 3 * g + V_TILE[t]), BLOCK * g - V_LANE[t]) for g in range(4)]),
            )

    def put_z(level):
        face_z[level, 0] = pick([roll_lanes(field[level, i, 3], BLOCK * (i - 3)) for i in range(4)])
        face_z[level, 1] = pick([roll_lanes(field[level, i, 0], BLOCK * i) for i in range(4)])

    put_z(0)

    spread_k = lax.broadcasted_iota(jnp.int32, (16, 4 * LANES), 0)
    spread_lane = lax.broadcasted_iota(jnp.int32, (16, 4 * LANES), 1)
    spread = (spread_k == 4 * ((spread_lane % LANES) // BLOCK) + spread_lane // LANES).astype(jnp.float32)
    wide = jnp.dot(
        w_ref[...].reshape(192, 16), spread, precision=lax.Precision.HIGHEST, preferred_element_type=jnp.float32
    )
    for d in range(3):
        for i in range(4):
            for t in range(4):
                r = 16 * (4 * d + i)
                value = wide[r : r + 16, t * LANES : (t + 1) * LANES] * (1.0 / WIDTH)
                weight[d, i, t] = value
                if d == 1:
                    face_wy[4 * i + t : 4 * i + t + 1, :] = value[15:16, :]

    pl.semaphore_wait(barrier, 6)

    def halo_copies(level):
        def copy(src, dst, n, device):
            return pltpu.make_async_remote_copy(
                src_ref=src,
                dst_ref=dst,
                send_sem=halo_send.at[level, n],
                recv_sem=halo_recv.at[level, n],
                device_id=device,
                device_id_type=MESH,
            )

        return [
            copy(field.at[level, 3], halo_x.at[level, 0], 0, beside("gx", 1)),
            copy(field.at[level, 0], halo_x.at[level, 1], 1, beside("gx", -1)),
            copy(face_z.at[level, 0], halo_z.at[level, 0], 2, beside("gz", 1)),
            copy(face_z.at[level, 1], halo_z.at[level, 1], 3, beside("gz", -1)),
            copy(face_y.at[level, 0], halo_y.at[level, 0], 4, beside("gy", 1)),
            copy(face_y.at[level, 1], halo_y.at[level, 1], 5, beside("gy", -1)),
        ]

    def edge_copy(src, dst, n, axis):
        return pltpu.make_async_remote_copy(
            src_ref=src,
            dst_ref=dst,
            send_sem=edge_send.at[n],
            recv_sem=edge_recv.at[n],
            device_id=beside(axis, 1),
            device_id_type=MESH,
        )

    edges = [
        edge_copy(weight.at[0, 3], edge_x, 0, "gx"),
        edge_copy(weight.at[2, :, 3], edge_z, 1, "gz"),
        edge_copy(face_wy, edge_y, 2, "gy"),
    ]
    rounds = [halo_copies(level) for level in range(POWERS)]
    for copy in edges + rounds[0]:
        copy.start()

    for i in range(4):
        rows = slice(16 * i, 16 * i + 16)
        for g in range(4):
            a, b, c = (q_tile(i, 3 * g + n) for n in range(3))
            pairs = [
                roll_lanes(a, 64),
                roll_lanes(jnp.where(lane >= 96, a, b), 96),
                b,
                roll_lanes(c, 32),
            ]
            for t in range(4):
                y_ref[4 * g + t, rows, :] = pairs[t]
                xb_ref[4 * g + t, rows, :] = roll_lanes(field[0, i, t], BLOCK * (2 - g))

    for copy in edges:
        copy.wait_recv()
    low_x, high_x = gx > 0, gx < nx - 1
    low_y, high_y = gy > 0, gy < ny - 1
    low_z, high_z = gz > 0, gz < nz - 1

    def kept(flag):
        return jnp.where(flag, 1.0, 0.0).astype(jnp.float32)

    for i in range(4):
        for t in range(4):
            r = slice(4 * i + t, 4 * i + t + 1)
            xp, yp, zp = weight[0, i, t], weight[1, i, t], weight[2, i, t]
            if i > 0:
                xm = weight[0, i - 1, t]
            else:
                xm = edge_x[t] * kept(low_x)
                rim_x[0, t] = xm
            if i == 3:
                rim_x[1, t] = xp * kept(high_x)
            below = edge_y[r, :] * kept(low_y)
            rim_y[0, r, :] = below
            rim_y[1, r, :] = yp[15:16, :] * kept(high_y)
            ym = pltpu.roll(yp, 1, axis=0)
            ym_all = jnp.where(row == 0, below, ym)
            if t > 0:
                zm = zm_all = weight[2, i, t - 1]
            else:
                rim = jnp.where(group == 0, roll_lanes(edge_z[i], 32) * kept(low_z), 0.0)
                rim_z[0, i] = rim
                zm = jnp.where(group == 0, 0.0, roll_lanes(weight[2, i, 3], 32))
                zm_all = zm + rim
            if t == 3:
                rim_z[1, i] = jnp.where(group == 3, zp * kept(high_z), 0.0)
            coef[0, i, t] = ((xp + xm) + (yp + ym_all)) + (zp + zm_all) - CENTRE / WIDTH
            coef[1, i, t] = xp
            coef[2, i, t] = xm
            coef[3, i, t] = jnp.where(row == 15, 0.0, yp)
            coef[4, i, t] = jnp.where(row == 0, 0.0, ym)
            coef[5, i, t] = jnp.where(group == 3, 0.0, zp) if t == 3 else zp
            coef[6, i, t] = zm

    def apply_inside(level):
        for i in range(4):
            for t in range(4):
                centre = field[level, i, t]
                yp, ym = pltpu.roll(centre, 15, axis=0), pltpu.roll(centre, 1, axis=0)
                zp = field[level, i, t + 1] if t < 3 else roll_lanes(field[level, i, 0], 96)
                zm = field[level, i, t - 1] if t > 0 else roll_lanes(field[level, i, 3], 32)
                value = coef[0, i, t] * centre
                if i < 3:
                    value = value - coef[1, i, t] * field[level, i + 1, t]
                if i > 0:
                    value = value - coef[2, i, t] * field[level, i - 1, t]
                value = value - (coef[3, i, t] * yp + coef[4, i, t] * ym)
                value = value - (coef[5, i, t] * zp + coef[6, i, t] * zm)
                if level > 0:
                    value = value - field[level - 1, i, t]
                field[level + 1, i, t] = value

    def apply_faces(level):
        for copy in rounds[level]:
            copy.wait_recv()
        following = rounds[level + 1] if level + 1 < POWERS else []
        low = rim_y[0] * halo_y[level, 0]
        high = rim_y[1] * halo_y[level, 1]
        for i in (3, 0, 1, 2):
            for t in range(4):
                r = slice(4 * i + t, 4 * i + t + 1)
                value = field[level + 1, i, t]
                if i == 3:
                    value = value - rim_x[1, t] * halo_x[level, 1, t]
                if i == 0:
                    value = value - rim_x[0, t] * halo_x[level, 0, t]
                value = value - jnp.where(row == 0, low[r, :], jnp.where(row == 15, high[r, :], 0.0))
                if t == 3:
                    value = value - rim_z[1, i] * roll_lanes(halo_z[level, 1], BLOCK * (3 - i))
                if t == 0:
                    value = value - rim_z[0, i] * roll_lanes(halo_z[level, 0], -BLOCK * i)
                put(level + 1, i, t, value)
            if i == 0:
                for copy in following[:2]:
                    copy.start()
        if following:
            put_z(level + 1)
        for copy in following[2:]:
            copy.start()

    def prepare(m):
        for i in range(4):
            rows = slice(16 * i, 16 * i + 16)
            for g in range(4):
                for t in range(4):
                    k = 4 * g + t
                    y_ref[k, rows, :] = jnp.where(
                        group == 1, roll_lanes(field[m - 1, i, t], BLOCK * (1 - g)), y_ref[k, rows, :]
                    )

    def products(m):
        for i in range(4):
            rows = slice(16 * i, 16 * i + 16)
            for g in range(4):
                for t in range(4):
                    k = 4 * g + t
                    y_ref[k, rows, :] = jnp.where(group == 0, roll_lanes(field[m, i, t], -BLOCK * g), y_ref[k, rows, :])
        y = y_ref[...].reshape(1024, LANES)
        return lax.dot_general(
            y if m == 1 else y[:, :BLOCK],
            y,
            (((0,), (0,)), ((), ())),
            precision=lax.Precision.HIGH,
            preferred_element_type=jnp.float32,
        )

    class Stream:
        def __init__(self, n, rows, refs):
            self.n, self.chunk = n, rows // nx
            self.local, self.part_x, self.part_z, self.part_y, self.total = (
                refs.at[pl.ds(8 * q, 8)] for q in range(5)
            )
            self.whole = refs.at[40]

        def copy(self, src, dst, phase, device):
            return pltpu.make_async_remote_copy(
                src_ref=src,
                dst_ref=dst,
                send_sem=sum_send.at[self.n, phase],
                recv_sem=sum_recv.at[self.n, phase],
                device_id=device,
                device_id_type=MESH,
            )

        def all_of(self, ref, phase):
            axis = ("gx", "gz", "gy", "gx")[phase]
            part = ref.at[pl.ds(1, size_of[axis] - 1)]
            return self.copy(part, part, phase, partner(axis, 1))

        def begin(self, values):
            for c in range(nx):
                self.local[c] = values[c * self.chunk : (c + 1) * self.chunk, :]
            for d in range(1, nx):
                self.copy(self.local.at[gx ^ d], self.part_x.at[d], 0, partner("gx", d)).start()
            self.part_x[0] = self.local[gx]

        def over_z(self):
            self.all_of(self.part_x, 0).wait_recv()
            self.part_z[0] = tree_sum([self.part_x[d] for d in range(nx)])
            for d in range(1, nz):
                self.copy(self.part_z.at[0], self.part_z.at[d], 1, partner("gz", d)).start()

        def over_y(self):
            self.all_of(self.part_z, 1).wait_recv()
            self.part_y[0] = tree_sum([self.part_z[d] for d in range(nz)])
            for d in range(1, ny):
                self.copy(self.part_y.at[0], self.part_y.at[d], 2, partner("gy", d)).start()

        def gather(self):
            self.all_of(self.part_y, 2).wait_recv()
            self.whole[...] = tree_sum([self.part_y[d] for d in range(ny)])
            for d in range(1, nx):
                self.copy(self.whole, self.total.at[gx], 3, partner("gx", d)).start()
            self.total[gx] = self.whole[...]

        def result(self):
            self.all_of(self.total, 3).wait_recv()
            for c in range(nx):
                gathered[c * self.chunk : (c + 1) * self.chunk, :] = self.total[c]
            return gathered[0 : nx * self.chunk, :] * (1.0 / (1024 * nx * ny * nz))

        def drain(self):
            for phase, ref in enumerate((self.part_x, self.part_z, self.part_y, self.total)):
                self.all_of(ref, phase).wait_send()

    a = Stream(0, LANES, stream_a)
    s2, s3, s4 = (Stream(n, BLOCK, ref) for n, ref in ((1, stream_2), (2, stream_3), (3, stream_4)))

    t, tau = scalars(shift_ref[0])
    done = dict(coef=[], inverse=[], back=[])
    known = {}
    eliminate = eliminate_in(rows_ref)

    def block(m, values, prior):
        out = level_algebra(m, values, known, done, prior, tau, eliminate)
        rows = slice(BLOCK * (m - 1), BLOCK * m)
        maps_ref[rows, :] = out["maps"]
        small_ref[0, rows, :] = out["factor"]
        small_ref[1, rows, :] = out["upper"]
        small_ref[2, rows, :] = out["twice"]

    apply_inside(0)
    prepare(1)
    apply_faces(0)
    for axis in AXES:
        for step in (2, -2):
            pl.semaphore_signal(ready_sem, inc=1, device_id=beside(axis, step), device_id_type=MESH)
    apply_inside(1)
    first = products(1)
    prepare(2)
    pl.semaphore_wait(ready_sem, 6)
    a.begin(first)
    apply_faces(1)
    apply_inside(2)
    a.over_z()
    s2.begin(products(2))
    xa_ref[...] = y_ref[...]
    prepare(3)
    apply_faces(2)
    apply_inside(3)
    a.over_y()
    s2.over_z()
    s3.begin(products(3))
    prepare(4)
    apply_faces(3)
    s4.begin(products(4))
    a.gather()
    s2.over_y()
    s3.over_z()
    for k in range(16):
        wide_lane = lax.broadcasted_iota(jnp.int32, (64, LANES), 1)
        xb_ref[k] = jnp.where(wide_lane < 64, y_ref[k], xb_ref[k])
    s4.over_z()
    gram = a.result()
    known[0] = (gram[32:64, :], 1)
    prior = prior_algebra(gram, tau)
    small_ref[3] = prior["off2"]
    s2.gather()
    s3.over_y()
    block(1, gram[:BLOCK, :], prior)
    s4.over_y()
    s3.gather()
    block(2, s2.result(), prior)
    s4.gather()
    block(3, s3.result(), prior)
    block(4, s4.result(), prior)

    for copy in edges + [c for r in rounds for c in r]:
        copy.wait_send()
    for stream in (a, s2, s3, s4):
        stream.drain()


def basis_kernel(xa_ref, xb_ref, maps_ref, small_ref, shift_ref, new_ref, projection_ref, triangle_ref):
    maps = maps_ref[...]
    for k in range(16):
        both = jnp.concatenate([xa_ref[k], xb_ref[k]], axis=1)
        out = lax.dot_general(
            both,
            maps,
            (((1,), (1,)), ((), ())),
            precision=lax.Precision.HIGH,
            preferred_element_type=jnp.float32,
        )
        for i in range(4):
            new_ref[i, :, k * LANES : (k + 1) * LANES] = out[16 * i : 16 * i + 16, :]
    t, _ = scalars(shift_ref[0])
    projection, triangle = small_outputs(small_ref[0], small_ref[1], small_ref[2], small_ref[3], t)
    projection_ref[0:64, :] = projection[64:, :]
    projection_ref[64:96, :] = projection[32:64, :]
    triangle_ref[...] = triangle


def per_device(sizes, prior_basis, edge_weights, spectral_shift):
    nx, ny, nz = sizes
    f32 = jnp.float32
    tile = (4, 16, LANES)
    vmem = pl.BlockSpec(memory_space=pltpu.VMEM)
    smem = pl.BlockSpec(memory_space=pltpu.SMEM)
    hbm = pl.BlockSpec(memory_space=pltpu.HBM)
    xa, xb, maps, small = pl.pallas_call(
        functools.partial(powers_kernel, sizes),
        out_shape=(
            jax.ShapeDtypeStruct((16, 64, LANES), f32),
            jax.ShapeDtypeStruct((16, 64, LANES), f32),
            jax.ShapeDtypeStruct((LANES, 2 * LANES), f32),
            jax.ShapeDtypeStruct((4, LANES, LANES), f32),
        ),
        in_specs=[hbm, hbm, smem],
        out_specs=(vmem,) * 4,
        scratch_shapes=[
            pltpu.VMEM((4, 16, 16 * BASIS), f32),
            pltpu.VMEM((3, 4, 16, 16), f32),
            pltpu.VMEM((16, 64, LANES), f32),
            pltpu.VMEM((POWERS + 1, 4, *tile), f32),
            pltpu.VMEM((3, 4, *tile), f32),
            pltpu.VMEM((7, 4, *tile), f32),
            pltpu.VMEM((2, *tile), f32),
            pltpu.VMEM((2, 16, LANES), f32),
            pltpu.VMEM((2, *tile), f32),
            pltpu.VMEM((POWERS, 2, *tile), f32),
            pltpu.VMEM((POWERS, 2, 16, LANES), f32),
            pltpu.VMEM((POWERS, 2, 16, LANES), f32),
            pltpu.VMEM((POWERS, 2, 16, LANES), f32),
            pltpu.VMEM((POWERS, 2, 16, LANES), f32),
            pltpu.VMEM(tile, f32),
            pltpu.VMEM((16, LANES), f32),
            pltpu.VMEM(tile, f32),
            pltpu.VMEM((16, LANES), f32),
            pltpu.VMEM((BLOCK, LANES), f32),
            pltpu.VMEM((LANES, LANES), f32),
            pltpu.VMEM((41, LANES // nx, LANES), f32),
            pltpu.VMEM((41, BLOCK // nx, LANES), f32),
            pltpu.VMEM((41, BLOCK // nx, LANES), f32),
            pltpu.VMEM((41, BLOCK // nx, LANES), f32),
            pltpu.SemaphoreType.DMA((2,)),
            pltpu.SemaphoreType.DMA((POWERS, 6)),
            pltpu.SemaphoreType.DMA((POWERS, 6)),
            pltpu.SemaphoreType.DMA((3,)),
            pltpu.SemaphoreType.DMA((3,)),
            pltpu.SemaphoreType.DMA((4, 4)),
            pltpu.SemaphoreType.DMA((4, 4)),
            pltpu.SemaphoreType.REGULAR,
        ],
        name="powers",
        compiler_params=pltpu.CompilerParams(
            collective_id=0, has_side_effects=True, vmem_limit_bytes=40 * 2**20
        ),
    )(
        pltpu.with_memory_space_constraint(prior_basis, pltpu.HBM),
        pltpu.with_memory_space_constraint(edge_weights, pltpu.HBM),
        spectral_shift,
    )
    return pl.pallas_call(
        basis_kernel,
        out_shape=(
            jax.ShapeDtypeStruct((4, 16, 16 * LANES), f32),
            jax.ShapeDtypeStruct((BASIS, LANES), f32),
            jax.ShapeDtypeStruct((LANES, LANES), f32),
        ),
        in_specs=[vmem, vmem, vmem, vmem, smem],
        out_specs=(vmem, vmem, vmem),
        name="basis",
        compiler_params=pltpu.CompilerParams(vmem_limit_bytes=32 * 2**20),
    )(xa, xb, maps, small, spectral_shift)


def solution(mesh):
    sizes = tuple(mesh.shape[a] for a in AXES)
    return jax.shard_map(
        functools.partial(per_device, sizes),
        mesh=mesh,
        in_specs=(P("gx", "gy", "gz"), P(None, "gx", "gy", "gz"), P()),
        out_specs=(P("gx", "gy", "gz"), P(), P()),
        check_vma=False,
    )
```
